512 devices in a mesh: grid: 64 (over y, z_hi, core), hel: 8 (over z_lo, x).
Axes of the slice: x: 4, y: 8, z: 8 (z_hi: 4, z_lo: 2; z = z_hi * 2 + z_lo), core: 2. Of those that a mesh axis runs over, the one named last changes fastest.
Arguments:
- packet_prev: float32 [8, 1024, 5120], P('hel', 'grid'), may hold values from -6 to 6
- packet_now: float32 [8, 1024, 5120], P('hel', 'grid'), may hold values from -6 to 6
- angular_table: float32 [8, 1024, 1536], P('hel', None, 'grid'), may hold values from -0.15625 to 0.15625
- potential: float32 [1536, 5120], P(None, 'grid'), may hold values from 0 to 2
- rotation: float32 [8, 1024], P('hel', 'grid'), may hold values from 0.05 to 1
- radial_weight: float32 [64], replicated, may hold values from 0.5 to 2
- coupling: float32 [8, 1024], P('hel', 'grid'), may hold values from -0.6 to 0.6
- centrifugal: float32 [80], replicated, may hold values from 0.5 to 1.5
Outputs:
- packet_mid: float32 [8, 1024, 5120], P('hel', 'grid')
- packet_last: float32 [8, 1024, 5120], P('hel', 'grid')
The draws below stay inside these ranges and needn't reach their ends.
All inputs are finite; a program needn't handle non-finite values.
Results may differ from the reference program's by a relative error of at most 0.0001.
Values sent between devices are 32-bit elements; how exact they have to be, the bound alone decides.
A program may use at most 128 MiB of HBM per device.

```python
import math
import jax
import jax.numpy as jnp
from jax import lax

J = 1024
Q = 1536
RB = 80
RS = 64
STEPS = 2
K = 8
NR = 5120


def levels(key, shape, cuts, least, largest):
    def one(axis_at, parts):
        heights = jax.random.uniform(jax.random.fold_in(jax.random.fold_in(key, 6), axis_at), (parts,), jnp.float32, least / len(cuts), largest / len(cuts))
        return jnp.repeat(jnp.exp(heights), shape[axis_at] // parts).reshape((-1,) + (1,) * (len(shape) - axis_at - 1))

    factor_of = one(*cuts[0])
    for cut in cuts[1:]:
        factor_of = factor_of * one(*cut)
    return factor_of


def gaussian(own_key, shape, spread, most, pieces=(), kind=jnp.bfloat16):
    loudness = levels(own_key, shape, pieces, -0.22, 0.18) if pieces else 1.0
    drawn = jax.random.normal(own_key, shape, jnp.float32) * spread * loudness
    return jnp.minimum(jnp.maximum(drawn, -most), most).astype(kind)


def setup_inputs(seed: int = 0) -> dict:
    arg_keys = jax.random.split(jax.random.key(seed), 9)
    packet_prev = gaussian(arg_keys[0], (K, J, NR), 1.0, 6.0, ((0, 8), (1, 64)), jnp.float32)
    packet_now = gaussian(arg_keys[1], (K, J, NR), 1.0, 6.0, ((0, 8), (1, 64)), jnp.float32)
    angular_table = gaussian(arg_keys[2], (K, J, Q), Q ** -0.5, 0.15625, ((0, 8), (2, 64)), jnp.float32)
    potential = jnp.clip(2.0 * jax.random.uniform(arg_keys[3], (Q, NR), jnp.float32) ** levels(arg_keys[3], (Q, NR), ((1, 64),), -0.2, 0.2), 0.0, 2.0)
    rotation = jnp.clip(jnp.exp(math.log(1.0) - 2.9957323 * jax.random.uniform(arg_keys[4], (K, J), jnp.float32) ** levels(arg_keys[4], (K, J), ((0, 8), (1, 64)), -0.2, 0.2)), 0.05, 1.0)
    radial_weight = jnp.clip(jax.random.uniform(arg_keys[5], (RS,), jnp.float32, 0.5, 2.0), 0.5, 2.0)
    coupling = jnp.clip(jax.random.uniform(arg_keys[6], (K, J), jnp.float32, -0.6, 0.6) * levels(arg_keys[6], (K, J), ((0, 8), (1, 64)), -0.4, 0.0), -0.6, 0.6)
    centrifugal = jnp.clip(jax.random.uniform(arg_keys[7], (RB,), jnp.float32, 0.5, 1.5), 0.5, 1.5)
    return dict(packet_prev=packet_prev, packet_now=packet_now, angular_table=angular_table, potential=potential, rotation=rotation, radial_weight=radial_weight, coupling=coupling, centrifugal=centrifugal)


big_scale = 0.05
small_scale = 0.08
centre = 1.0
half_width = 1.5


def kinetic(count, coef):
    index = jnp.arange(count)
    offset = index[:, None] - index[None, :]
    parity = (1 - 2 * (jnp.abs(offset) % 2)).astype(jnp.float32)
    square = jnp.maximum(offset * offset, 1).astype(jnp.float32)
    return coef * jnp.where(offset == 0, jnp.float32(jnp.pi ** 2 / 3.0), 2.0 * parity / square)


def hamiltonian(packet, angular_table, potential, rotation, radial_weight, coupling, centrifugal, kin_big, kin_small):
    high = lax.Precision.HIGHEST
    grid4 = packet.reshape(K, J, RB, RS)
    radial = jnp.einsum('ab,kjbs->kjas', kin_big, grid4, precision=high)
    radial = radial + jnp.einsum('st,kjat->kjas', kin_small, grid4, precision=high)
    radial = radial.reshape(K, J, NR)
    rotational = rotation[:, :, None] * jnp.tile(radial_weight, RB)[None, None, :] * packet
    points = jnp.einsum('kjq,kjn->kqn', angular_table, packet, precision=high)
    back = jnp.einsum('kjq,kqn->kjn', angular_table, points * potential[None], precision=high)
    link = coupling[:, :, None] * jnp.repeat(centrifugal, RS)[None, None, :]
    zeros = jnp.zeros_like(packet[:1])
    below = jnp.concatenate([zeros, packet[:-1]], axis=0)
    scaled = link * packet
    above = jnp.concatenate([scaled[1:], zeros], axis=0)
    coriolis = link * below + above
    return (radial + rotational + back + coriolis - centre * packet) / half_width


def reference(packet_prev, packet_now, angular_table, potential, rotation, radial_weight, coupling, centrifugal):
    kin_big = kinetic(RB, big_scale)
    kin_small = kinetic(RS, small_scale)
    older, newer = packet_prev, packet_now
    for step in range(STEPS):
        applied = hamiltonian(newer, angular_table, potential, rotation, radial_weight, coupling, centrifugal, kin_big, kin_small)
        older, newer = newer, 2.0 * applied - older
    return older, newer
```

```python
import jax
import jax.numpy as jnp
from jax import lax
from jax.sharding import Mesh
from jax.sharding import PartitionSpec as P
from jax.experimental import pallas as pl
from jax.experimental.pallas import tpu as pltpu

RB = 80
RS = 64
STEPS = 2
GRID = ("grid_0", "grid_1", "grid_2")


big_scale = 0.05
small_scale = 0.08
centre = 1.0
half_width = 1.5


def in_order(parts, dim):
    parts = jnp.moveaxis(parts, 0, dim)
    lengths = parts.shape
    return parts.reshape(*lengths[:dim], lengths[dim] * lengths[dim + 1], *lengths[dim + 2 :])


def stacked_from(shard, axes, sequence):
    parts = shard[None]
    for k in sequence:
        parts = lax.all_gather(parts, axes[k], axis=0, tiled=True)
    carried = [lax.axis_size(axes[k]) for k in reversed(sequence)]
    parts = parts.reshape(*carried, *shard.shape)
    turned = sorted(range(len(sequence)), key=lambda place: sequence[len(sequence) - 1 - place])
    return parts.transpose(*turned, *range(len(sequence), parts.ndim)).reshape(-1, *shard.shape)


def whole_of(shard, axes, sequence, dim):
    return in_order(stacked_from(shard, axes, sequence), dim)


def from_behind(shard, axis, by):
    size = lax.axis_size(axis)
    pairs = [(i, i + by) for i in range(size) if 0 <= i + by < size]
    return lax.ppermute(shard, axis, pairs)


def kinetic(count, coef):
    index = jnp.arange(count)
    offset = index[:, None] - index[None, :]
    parity = (1 - 2 * (jnp.abs(offset) % 2)).astype(jnp.float32)
    square = jnp.maximum(offset * offset, 1).astype(jnp.float32)
    return coef * jnp.where(offset == 0, jnp.float32(jnp.pi**2 / 3.0), 2.0 * parity / square)


def swap_kernel(x_ref, o_ref, send_sem, recv_sem, own_sem):
    y, z, c, h = [lax.axis_index(a) for a in GRID + ("hel",)]
    me = (y * 4 + z) * 2 + c

    def peer(d):
        return (d // 8, lax.rem(d // 2, 4), lax.rem(d, 2), h)

    barrier = pltpu.get_barrier_semaphore()

    @pl.loop(1, 64)
    def _(i):
        pl.semaphore_signal(barrier, inc=1, device_id=peer(lax.rem(me + i, 64)), device_id_type=pl.DeviceIdType.MESH)

    own = pltpu.make_async_copy(x_ref.at[me], o_ref.at[me], own_sem)
    own.start()
    pl.semaphore_wait(barrier, 63)

    @pl.loop(1, 64)
    def _(i):
        d = lax.rem(me + i, 64)
        pltpu.make_async_remote_copy(
            src_ref=x_ref.at[d], dst_ref=o_ref.at[me], send_sem=send_sem, recv_sem=recv_sem,
            device_id=peer(d), device_id_type=pl.DeviceIdType.MESH,
        ).start()

    own.wait()
    pltpu.make_async_remote_copy(
        src_ref=x_ref.at[pl.ds(0, 63)], dst_ref=o_ref.at[pl.ds(0, 63)], send_sem=send_sem, recv_sem=recv_sem,
        device_id=peer(lax.rem(me + 1, 64)), device_id_type=pl.DeviceIdType.MESH,
    ).wait()


def swap(x):
    return pl.pallas_call(
        swap_kernel,
        out_shape=jax.ShapeDtypeStruct(x.shape, x.dtype),
        in_specs=[pl.BlockSpec(memory_space=pltpu.VMEM)],
        out_specs=pl.BlockSpec(memory_space=pltpu.VMEM),
        scratch_shapes=[pltpu.SemaphoreType.DMA, pltpu.SemaphoreType.DMA, pltpu.SemaphoreType.DMA],
        compiler_params=pltpu.CompilerParams(collective_id=0, has_side_effects=True),
    )(x)


def shards(
    packet_prev,
    packet_now,
    angular_table,
    potential,
    rotation,
    radial_weight,
    coupling,
    centrifugal,
):
    high = lax.Precision.HIGHEST
    kin_big = kinetic(RB, big_scale)
    kin_small = kinetic(RS, small_scale)
    whole_table = whole_of(angular_table, GRID, (1, 0, 2), 2)[0]
    link = coupling[:, :, None] * jnp.repeat(centrifugal, RS)[None, None, :]
    rot_factor = rotation[:, :, None] * jnp.tile(radial_weight, RB)[None, None, :]
    older, newer = (packet_prev, packet_now)
    for step in range(STEPS):
        local_funcs = newer.shape[1]
        grid4 = newer.reshape(1, local_funcs, RB, RS)
        radial = jnp.einsum("ab,kjbs->kjas", kin_big, grid4, precision=high)
        radial = radial + jnp.einsum("st,kjat->kjas", kin_small, grid4, precision=high)
        radial = radial.reshape(newer.shape)
        below = from_behind(newer, "hel", 1)
        above = from_behind(link * newer, "hel", -1)
        spread = swap(newer[0].reshape(16, 64, 80).transpose(1, 0, 2)).reshape(1024, 80)
        points = lax.dot_general(whole_table, spread, (((0,), (0,)), ((), ())), precision=high)
        back = jnp.dot(whole_table, points * potential, precision=high)
        returned = swap(back.reshape(64, 16, 80)).transpose(1, 0, 2).reshape(1, 16, 5120)
        total = radial + rot_factor * newer + returned + link * below + above
        older, newer = (newer, 2.0 * ((total - centre * newer) / half_width) - older)
    return (older, newer)


def solution(mesh):
    finer = Mesh(
        mesh.devices.reshape(8, 4, 2, mesh.shape["hel"]), ("grid_0", "grid_1", "grid_2", "hel")
    )
    placed = (
        P("hel", GRID, None),
        P("hel", GRID, None),
        P("hel", None, GRID),
        P(None, GRID),
        P("hel", GRID),
        P(),
        P("hel", GRID),
        P(),
    )
    return jax.shard_map(
        shards,
        mesh=finer,
        in_specs=placed,
        out_specs=(P("hel", GRID, None), P("hel", GRID, None)),
        check_vma=False,
    )
```

```python
import functools

import jax
import jax.numpy as jnp
import numpy as np
from jax import lax
from jax.experimental import pallas as pl
from jax.experimental.pallas import tpu as pltpu
from jax.sharding import Mesh
from jax.sharding import PartitionSpec as P

RB = 80
RS = 64
J = 1024
Q = 1536
NB = 80
ROWS = 16
TILES = 40
MSG = 10
GRID = ("grid_0", "grid_1", "grid_2")
MESH = pl.DeviceIdType.MESH

big_scale = 0.05
small_scale = 0.08
centre = 1.0
half_width = 1.5
FACTOR = 2.0 / half_width


def kinetic_entry(offset, coef):
    offset = np.asarray(offset, np.int64)
    parity = 1 - 2 * (np.abs(offset) % 2)
    square = np.maximum(offset * offset, 1)
    return (coef * np.where(offset == 0, np.pi**2 / 3.0, 2.0 * parity / square)).astype(np.float32)


def kinetic_tables():
    index = np.arange(RS)
    small = kinetic_entry(index[:, None] - index[None, :], small_scale)
    pair = np.zeros((128, 128), np.float32)
    pair[:64, :64] = small
    pair[64:, 64:] = small
    apart = 2 * (np.arange(80) - 39)
    same = np.broadcast_to(kinetic_entry(apart, big_scale)[:, None, None], (80, 8, 128))
    half = np.where(np.arange(128) < 64, -1, 1)
    other = kinetic_entry(apart[:, None] + half[None, :], big_scale)
    return pair, np.ascontiguousarray(same), np.ascontiguousarray(np.broadcast_to(other[:, None, :], (80, 8, 128)))


def lanes(shape=(8, 128)):
    return lax.broadcasted_iota(jnp.int32, shape, 1)


def turn(x, shift, axis):
    shift = shift % x.shape[axis]
    return x if shift == 0 else pltpu.roll(x, shift, axis)


def swap_blocks(x):
    row = lax.broadcasted_iota(jnp.int32, (16, 128), 0) // 2
    lane = lanes((16, 128)) // 16
    apart = (row - lane + 8) % 8
    out = x
    for delta in range(1, 8):
        moved = turn(turn(x, 2 * delta, 0), -16 * delta, 1)
        out = jnp.where(apart == delta, moved, out)
    return out


def store_message(tx, place, main, swapped, i):
    tx[place, 0:8, :] = main
    half = swapped[0:8] if i < 4 else swapped[8:16]
    tx[place, 8:16, :] = turn(half, -2 * (i % 4), 0)


def load_swapped(rx, first):
    row = lax.broadcasted_iota(jnp.int32, (8, 128), 0) // 2
    halves = []
    for top in range(2):
        out = None
        for i in range(4):
            tile = turn(rx[first + 4 * top + i, 8:16, :], 2 * i, 0)
            out = tile if out is None else jnp.where(row == i, tile, out)
        halves.append(out)
    return jnp.concatenate(halves, axis=0)


def pack_columns(src, tx, group):
    lane = lanes()
    rows = []
    for half in range(2):
        rows.append(
            [src[8 * half : 8 * half + 8, pl.ds(pl.multiple_of(group * 640 + 128 * t, 128), 128)] for t in range(5)]
        )

    def piece(tiles, start, to):
        t, o = start // 128, start % 128
        x = tiles[t]
        if o > 64:
            x = jnp.where(lane >= o, x, tiles[t + 1])
        return turn(x, to - o, 1)

    rests = []
    for half in range(2):
        out = None
        for i in range(8):
            t, o = (80 * i + 64) // 128, (80 * i + 64) % 128
            x = turn(rows[half][t], 16 * i - o, 1)
            out = x if out is None else jnp.where(lane // 16 == i, x, out)
        rests.append(out)
    swapped = swap_blocks(jnp.concatenate(rests, axis=0))
    for i in range(8):
        main = jnp.where(lane < 64, piece(rows[0], 80 * i, 0), piece(rows[1], 80 * i, 64))
        store_message(tx, group * 8 + i, main, swapped, i)


def unpack_columns(rx, group):
    lane = lanes()
    rest = swap_blocks(load_swapped(rx, group * 8))
    out = [[None] * 5, [None] * 5]
    mains = [rx[group * 8 + i, 0:8, :] for i in range(8)]
    for half in range(2):
        part = rest[8 * half : 8 * half + 8]
        for t in range(5):
            x = jnp.zeros((8, 128), jnp.float32)
            for i in range(8):
                first = 80 * i - 128 * t
                if first + 64 > 0 and first < 128:
                    moved = turn(mains[i], first - 64 * half, 1)
                    x = jnp.where((lane >= first) & (lane < first + 64), moved, x)
                first = 80 * i + 64 - 128 * t
                if first >= 0 and first < 128:
                    moved = turn(part, first - 16 * i, 1)
                    x = jnp.where((lane >= first) & (lane < first + 16), moved, x)
            out[half][t] = x
    return [jnp.concatenate([out[0][t], out[1][t]], axis=0) for t in range(5)]


def unpack_rows(rx, group):
    lane = lanes()
    rest = swap_blocks(load_swapped(rx, group * 8))
    blocks = []
    for i in range(8):
        main = rx[group * 8 + i, 0:8, :]
        for half in range(2):
            part = turn(rest[8 * half : 8 * half + 8], 64 - 16 * i, 1)
            x = jnp.where(lane < 64, turn(main, 64 * half, 1), part)
            blocks.append(jnp.where(lane < 80, x, 0.0))
    return jnp.concatenate(blocks, axis=0)


def pack_rows(x, tx, group):
    lane = lanes()
    rests = []
    for half in range(2):
        out = None
        for i in range(8):
            part = turn(x[16 * i + 8 * half : 16 * i + 8 * half + 8], 16 * i - 64, 1)
            out = part if out is None else jnp.where(lane // 16 == i, part, out)
        rests.append(out)
    swapped = swap_blocks(jnp.concatenate(rests, axis=0))
    for i in range(8):
        main = jnp.where(lane < 64, x[16 * i : 16 * i + 8], turn(x[16 * i + 8 : 16 * i + 16], 64, 1))
        store_message(tx, group * 8 + i, main, swapped, i)


def halves_of(x):
    high = x.astype(jnp.bfloat16)
    return high, (x - high.astype(jnp.float32)).astype(jnp.bfloat16)


def column(ref, m):
    return ref[:, pl.ds(pl.multiple_of(m * 128, 128), 128)]


def kernel(
    p0, p1, tt, vt, rot, rw, cpl, cent, pair, same, other,
    mid, last,
    tall, thigh, tlow, vs, pt, spread, acc, scaled, below, above, linear,
    tx0, tx1, tx2, tx3, rx0, rx1, rx2, rx3,
    own_sem, t_send, z_recv, y_recv, c_recv, a_send, a_recv, h_send, h_recv, z_ready, c_ready,
):
    txs, rxs = (tx0, tx1, tx2, tx3), (rx0, rx1, rx2, rx3)
    y, z, c, h = [lax.axis_index(a) for a in GRID + ("hel",)]

    def slot(yy, zz, cc):
        return (yy * 4 + zz) * 2 + cc

    me = slot(y, z, c)
    up, down = (lax.rem(y + 1, 8), z, c, h), (lax.rem(y + 7, 8), z, c, h)
    twin = (y, z, 1 - c, h)
    y_line = [(lax.rem(y + i, 8), z, c, h) for i in range(1, 8)]
    z_line = [(y, lax.rem(z + i, 4), c, h) for i in range(1, 4)]
    higher, lower = (y, z, c, h + 1), (y, z, c, h - 1)

    barrier = pltpu.get_barrier_semaphore()
    for device in z_line + y_line + [twin]:
        pl.semaphore_signal(barrier, inc=1, device_id=device, device_id_type=MESH)

    @pl.when(h < 7)
    def _():
        pl.semaphore_signal(barrier, inc=1, device_id=higher, device_id_type=MESH)

    @pl.when(h > 0)
    def _():
        pl.semaphore_signal(barrier, inc=1, device_id=lower, device_id_type=MESH)

    def scale(src, step):
        @pl.loop(0, TILES)
        def _(m):
            link = cpl[...] * cent[pl.ds(m, 1), :]
            scaled[step, :, pl.ds(pl.multiple_of(m * 128, 128), 128)] = link * column(src, m)

    scale(p1, 0)
    own = pltpu.make_async_copy(tt, tall.at[me], own_sem)
    own.start()

    @pl.loop(0, 8)
    def _(group):
        pack_columns(p1, tx0, group)

    lane80 = lax.broadcasted_iota(jnp.int32, (NB, 128), 1)
    for yy in range(8):
        first = 192 * yy // 128
        a, b = vt[:, 128 * first : 128 * first + 128], vt[:, 128 * first + 128 : 128 * first + 256]
        if yy % 2:
            a, b = turn(a, 64, 1), turn(b, 64, 1)
            a = jnp.where(lane80 < 64, a, b)
        vs[yy, :, 0:128] = a
        vs[yy, :, 128:256] = b

    neighbours = 11 + (h > 0).astype(jnp.int32) + (h < 7).astype(jnp.int32)
    pl.semaphore_wait(barrier, neighbours)

    def block_copy(src, dst_slot, recv, device):
        return pltpu.make_async_remote_copy(
            src_ref=src, dst_ref=tall.at[dst_slot], send_sem=t_send, recv_sem=recv, device_id=device, device_id_type=MESH
        )

    def hel_copies(step, src):
        return (
            pltpu.make_async_remote_copy(
                src_ref=src, dst_ref=below.at[step], send_sem=h_send.at[step, 0], recv_sem=h_recv.at[step, 0],
                device_id=higher, device_id_type=MESH,
            ),
            pltpu.make_async_remote_copy(
                src_ref=scaled.at[step], dst_ref=above.at[step], send_sem=h_send.at[step, 1],
                recv_sem=h_recv.at[step, 1], device_id=lower, device_id_type=MESH,
            ),
        )

    def hel_start(step, src):
        to_higher, to_lower = hel_copies(step, src)

        @pl.when(h < 7)
        def _():
            to_higher.start()

        @pl.when(h > 0)
        def _():
            to_lower.start()

    def hel_wait(step, src):
        to_higher, to_lower = hel_copies(step, src)

        @pl.when(h > 0)
        def _():
            to_higher.wait_recv()
            to_lower.wait_send()

        @pl.when(h < 7)
        def _():
            to_lower.wait_recv()
            to_higher.wait_send()

        @pl.when(h == 0)
        def _():
            below[step] = jnp.zeros((ROWS, TILES * 128), jnp.float32)

        @pl.when(h == 7)
        def _():
            above[step] = jnp.zeros((ROWS, TILES * 128), jnp.float32)

    for i in range(1, 4):
        block_copy(tt, me, z_recv.at[i - 1], z_line[i - 1]).start()
    hel_start(0, p1)
    for device in z_line:
        pl.semaphore_signal(z_ready, inc=1, device_id=device, device_id_type=MESH)

    def pass_on(dy, zz, src, ahead, behind):
        place = slot(lax.rem(y + dy + 8, 8), zz, c)
        if ahead is not None:
            block_copy(src, place, y_recv.at[0, ahead, zz], up).start()
        if behind is not None:
            block_copy(src, place, y_recv.at[1, behind, zz], down).start()
        block_copy(src, place, c_recv.at[(dy + 8) % 8, zz], twin).start()

    def arrived(recv):
        block_copy(tall.at[0], 0, recv, twin).wait_recv()

    def exchange_start(k, group, dy):
        tx, rx = txs[k], rxs[k]

        @pl.loop(0, 8)
        def _(e):
            zz, cc = lax.rem(z + e // 2, 4), lax.rem(c + lax.rem(e, 2), 2)
            to = slot(group, zz, cc)
            itself = (dy == 0) & (e == 0)

            @pl.when(jnp.logical_not(itself))
            def _():
                pltpu.make_async_remote_copy(
                    src_ref=tx.at[to, pl.ds(0, MSG)], dst_ref=rx.at[me, pl.ds(0, MSG)],
                    send_sem=a_send.at[k], recv_sem=a_recv.at[k, lax.rem(8 - dy, 8)],
                    device_id=(group, zz, cc, h), device_id_type=MESH,
                ).start()

            @pl.when(itself)
            def _():
                rx[me] = tx[me]

    def far_first(i):
        return lax.rem(jnp.where(lax.rem(i, 2) == 1, 4 - (i + 1) // 2, 4 + i // 2), 8)

    def exchange_wait(k, dy):
        tx, rx = txs[k], rxs[k]

        def wait(count):
            pltpu.make_async_remote_copy(
                src_ref=tx.at[pl.ds(0, count), pl.ds(0, MSG)], dst_ref=rx.at[pl.ds(0, count), pl.ds(0, MSG)],
                send_sem=a_send.at[k], recv_sem=a_recv.at[k, dy], device_id=twin, device_id_type=MESH,
            ).wait_recv()

        @pl.when(dy == 0)
        def _():
            wait(7)

        @pl.when(dy != 0)
        def _():
            wait(8)

    def exchange_sent(k):
        pltpu.make_async_remote_copy(
            src_ref=txs[k].at[pl.ds(0, 63), pl.ds(0, MSG)], dst_ref=rxs[k].at[pl.ds(0, 63), pl.ds(0, MSG)],
            send_sem=a_send.at[k], recv_sem=a_recv.at[k, 0], device_id=twin, device_id_type=MESH,
        ).wait_send()

    def local_part(src, older):
        turned = rot[...] * rw[...] - centre

        @pl.loop(0, TILES // 8)
        def _(g):
            def add(m, sums):
                x = column(src, m)
                parts = []
                for half in range(2):
                    xh = x[8 * half : 8 * half + 8]
                    xs = turn(xh, 64, 1)
                    for u in range(8):
                        r = 8 * g + u - m + 39
                        parts.append(sums[8 * half + u] + same[r] * xh + other[r] * xs)
                return tuple(parts)

            sums = lax.fori_loop(0, TILES, add, tuple(jnp.zeros((8, 128), jnp.float32) for _ in range(16)))
            xs = [column(src, 8 * g + u) for u in range(8)]
            small = jnp.dot(
                jnp.concatenate(xs, axis=0), pair[...],
                precision=lax.Precision.HIGHEST, preferred_element_type=jnp.float32,
            )
            for u in range(8):
                whole = jnp.concatenate([sums[u], sums[8 + u]], axis=0) + small[16 * u : 16 * u + 16]
                at = pl.ds(pl.multiple_of((8 * g + u) * 128, 128), 128)
                linear[:, at] = FACTOR * (whole + turned * xs[u]) - older[:, at]

    def add_coriolis(step):
        @pl.loop(0, TILES)
        def _(m):
            at = pl.ds(pl.multiple_of(m * 128, 128), 128)
            link = cpl[...] * cent[pl.ds(m, 1), :]
            linear[:, at] = linear[:, at] + FACTOR * (link * below[step, :, at] + above[step, :, at])

    def table_halves(yy):
        table = tall[pl.ds(yy * 8, 8)].reshape(192, J)
        high, low = halves_of(table)
        thigh[yy] = high
        tlow[yy] = low

    nt = (((1,), (1,)), ((), ()))

    def potential_part(yy, first):
        both = lax.dot_general(pt[...], thigh[yy], nt, preferred_element_type=jnp.float32)
        cross = lax.dot_general(pt[0:NB], tlow[yy], nt, preferred_element_type=jnp.float32)
        points = (both[0:NB] + both[NB:] + cross) * vs[yy, :, 0:192]
        high, low = halves_of(points)
        both = jnp.dot(jnp.concatenate([high, low], axis=0), thigh[yy], preferred_element_type=jnp.float32)
        cross = jnp.dot(high, tlow[yy], preferred_element_type=jnp.float32)
        total = both[0:NB] + both[NB:] + cross
        if first:
            acc[0:NB] = total
        else:
            acc[0:NB] = acc[0:NB] + total

    own.wait()
    pl.semaphore_wait(z_ready, 3)
    pl.semaphore_signal(c_ready, inc=1, device_id=twin, device_id_type=MESH)
    pass_on(0, z, tall.at[me], 0, 0)
    pl.semaphore_wait(c_ready, 1)

    @pl.loop(0, 8)
    def _(i):
        dy = far_first(i)
        exchange_start(0, lax.rem(y + dy, 8), dy)

    for i in range(1, 4):
        arrived(z_recv.at[i - 1])
        zz = lax.rem(z + 4 - i, 4)
        pass_on(0, zz, tall.at[slot(y, zz, c)], 0, 0)

    local_part(p1, p0)

    def ring(s):
        for zz in range(4):
            place = slot(lax.rem(y + 8 - s, 8), zz, c)
            if s < 4 or zz < 2:
                arrived(y_recv.at[0, s - 1, zz])
                pass_on(-s, zz, tall.at[place], s if s < 3 or (s == 3 and zz < 2) else None, None)
            place = slot(lax.rem(y + s, 8), zz, c)
            if s < 4 or zz >= 2:
                arrived(y_recv.at[1, s - 1, zz])
                pass_on(s, zz, tall.at[place], None, s if s < 3 or (s == 3 and zz >= 2) else None)

    def compute(dy, first=False):
        for zz in range(4):
            arrived(c_recv.at[dy % 8, zz])
        yy = lax.rem(y + dy + 8, 8)
        table_halves(yy)
        potential_part(yy, first)

    hel_wait(0, p1)
    add_coriolis(0)
    ring(1)

    @pl.loop(0, 8)
    def _(i):
        dy = far_first(i)
        group = lax.rem(y + dy, 8)
        pack_columns(linear, tx1, group)
        exchange_start(1, group, dy)

    @pl.loop(0, 8)
    def _(dy):
        exchange_wait(0, dy)
        group = lax.rem(y + dy, 8)
        at = pl.ds(pl.multiple_of(group * 128, 128), 128)
        high, low = halves_of(unpack_rows(rx0, group).T[0:NB])
        pt[0:NB, at] = high
        pt[NB : 2 * NB, at] = low

    compute(0, True)
    ring(2)
    compute(1)
    compute(-1)
    ring(3)
    compute(2)
    compute(-2)
    ring(4)

    @pl.loop(0, 8)
    def _(dy):
        exchange_wait(1, dy)
        group = lax.rem(y + dy, 8)
        at = pl.ds(pl.multiple_of(group * 128, 128), 128)
        spread[:, at] = unpack_rows(rx1, group).T[0:NB]

    compute(3)
    compute(-3)
    compute(4)

    def send_back(k):
        @pl.loop(0, 8)
        def _(i):
            dy = far_first(i)
            group = lax.rem(y + dy, 8)
            at = pl.ds(pl.multiple_of(group * 128, 128), 128)
            pack_rows(acc[:, at].T, txs[k], group)
            exchange_start(k, group, dy)

    acc[NB:128] = jnp.zeros((128 - NB, J), jnp.float32)
    send_back(2)

    @pl.loop(0, 8)
    def _(group):
        at = pl.ds(pl.multiple_of(group * 128, 128), 128)
        high, low = halves_of(spread[:, at] + FACTOR * acc[0:NB, at])
        pt[0:NB, at] = high
        pt[NB : 2 * NB, at] = low

    potential_part(0, True)

    @pl.loop(1, 8)
    def _(yy):
        potential_part(yy, False)

    send_back(3)

    def take_back(k, out):
        @pl.loop(0, 8)
        def _(dy):
            exchange_wait(k, dy)
            group = lax.rem(y + dy, 8)
            for t, tile in enumerate(unpack_columns(rxs[k], group)):
                at = pl.ds(pl.multiple_of(group * 640 + 128 * t, 128), 128)
                out[:, at] = linear[:, at] + FACTOR * tile

    take_back(2, mid)
    scale(mid, 1)
    hel_start(1, mid)
    local_part(mid, p1)
    hel_wait(1, mid)
    add_coriolis(1)
    take_back(3, last)

    for k in range(4):
        exchange_sent(k)
    pltpu.make_async_remote_copy(
        src_ref=tall.at[pl.ds(0, 63)], dst_ref=tall.at[pl.ds(0, 63)], send_sem=t_send, recv_sem=z_recv.at[0],
        device_id=twin, device_id_type=MESH,
    ).wait_send()


def shards(packet_prev, packet_now, angular_table, potential, rotation, radial_weight, coupling, centrifugal):
    pair, same, other = (jnp.asarray(a) for a in kinetic_tables())
    whole = jax.ShapeDtypeStruct((ROWS, TILES * 128), jnp.float32)
    vmem = pl.BlockSpec(memory_space=pltpu.VMEM)
    packet = (ROWS, TILES * 128)
    f32, bf16 = jnp.float32, jnp.bfloat16
    dma = pltpu.SemaphoreType.DMA
    mid, last = pl.pallas_call(
        kernel,
        out_shape=(whole, whole),
        in_specs=[vmem] * 11,
        out_specs=(vmem, vmem),
        scratch_shapes=[
            pltpu.VMEM((64, 24, J), f32),
            pltpu.VMEM((8, 192, J), bf16),
            pltpu.VMEM((8, 192, J), bf16),
            pltpu.VMEM((8, NB, 256), f32),
            pltpu.VMEM((2 * NB, J), bf16),
            pltpu.VMEM((NB, J), f32),
            pltpu.VMEM((128, J), f32),
            pltpu.VMEM((2, *packet), f32),
            pltpu.VMEM((2, *packet), f32),
            pltpu.VMEM((2, *packet), f32),
            pltpu.VMEM(packet, f32),
            *[pltpu.VMEM((64, 16, 128), f32) for _ in range(8)],
            dma,
            dma,
            dma((3,)),
            dma((2, 4, 4)),
            dma((8, 4)),
            dma((4,)),
            dma((4, 8)),
            dma((2, 2)),
            dma((2, 2)),
            pltpu.SemaphoreType.REGULAR,
            pltpu.SemaphoreType.REGULAR,
        ],
        compiler_params=pltpu.CompilerParams(collective_id=0, has_side_effects=True, vmem_limit_bytes=56 << 20),
        cost_estimate=pl.CostEstimate(flops=4 * 3 * 2 * J * Q * NB, bytes_accessed=4 << 20, transcendentals=0),
    )(
        packet_prev[0],
        packet_now[0],
        angular_table[0].T,
        potential.T,
        rotation.reshape(ROWS, 1),
        jnp.tile(radial_weight, 2).reshape(1, 128),
        coupling.reshape(ROWS, 1),
        jnp.repeat(centrifugal, RS).reshape(TILES, 128),
        pair,
        same,
        other,
    )
    return mid[None], last[None]


def solution(mesh):
    finer = Mesh(
        mesh.devices.reshape(8, 4, 2, mesh.shape["hel"]), ("grid_0", "grid_1", "grid_2", "hel")
    )
    placed = (
        P("hel", GRID, None),
        P("hel", GRID, None),
        P("hel", None, GRID),
        P(None, GRID),
        P("hel", GRID),
        P(),
        P("hel", GRID),
        P(),
    )
    return jax.shard_map(
        shards,
        mesh=finer,
        in_specs=placed,
        out_specs=(P("hel", GRID, None), P("hel", GRID, None)),
        check_vma=False,
    )
```

```python
import functools

import jax
import jax.numpy as jnp
import numpy as np
from jax import lax
from jax.experimental import pallas as pl
from jax.experimental.pallas import tpu as pltpu
from jax.sharding import Mesh
from jax.sharding import PartitionSpec as P

RB = 80
RS = 64
J = 1024
Q = 1536
NB = 80
ROWS = 16
TILES = 40
MSG = 10
GRID = ("grid_0", "grid_1", "grid_2")
MESH = pl.DeviceIdType.MESH

big_scale = 0.05
small_scale = 0.08
centre = 1.0
half_width = 1.5
FACTOR = 2.0 / half_width


def kinetic_entry(offset, coef):
    offset = np.asarray(offset, np.int64)
    parity = 1 - 2 * (np.abs(offset) % 2)
    square = np.maximum(offset * offset, 1)
    return (coef * np.where(offset == 0, np.pi**2 / 3.0, 2.0 * parity / square)).astype(np.float32)


def two_halves(x):
    high = x.astype(jnp.bfloat16)
    return high, (x - high.astype(np.float32)).astype(jnp.bfloat16)


def kinetic_tables():
    index = np.arange(RS)
    pair = np.zeros((128, 128), np.float32)
    pair[:64, :64] = pair[64:, 64:] = kinetic_entry(index[:, None] - index[None, :], small_scale)
    high, low = two_halves(pair)
    small = np.concatenate([high, high, low], axis=0)
    apart = 2 * (np.arange(TILES)[:, None] - np.arange(TILES)[None, :])
    big = np.zeros((128, 48), np.float32)
    for i, more in enumerate((0, -1, 1)):
        big[40 * i : 40 * i + 40, :40] = kinetic_entry(apart + more, big_scale)
    high, low = two_halves(big)
    return small, np.concatenate([high, high, low], axis=1)


def lanes(shape=(8, 128)):
    return lax.broadcasted_iota(jnp.int32, shape, 1)


def turn(x, shift, axis):
    shift = shift % x.shape[axis]
    return x if shift == 0 else pltpu.roll(x, shift, axis)


def swap_blocks(x):
    row = lax.broadcasted_iota(jnp.int32, (16, 128), 0) // 2
    lane = lanes((16, 128)) // 16
    apart = (row - lane + 8) % 8
    out = x
    for delta in range(1, 8):
        moved = turn(turn(x, 2 * delta, 0), -16 * delta, 1)
        out = jnp.where(apart == delta, moved, out)
    return out


def store_message(tx, place, main, swapped, i):
    tx[place, 0:8, :] = main
    half = swapped[0:8] if i < 4 else swapped[8:16]
    tx[place, 8:16, :] = turn(half, -2 * (i % 4), 0)


def load_swapped(rx, first):
    row = lax.broadcasted_iota(jnp.int32, (8, 128), 0) // 2
    halves = []
    for top in range(2):
        out = None
        for i in range(4):
            tile = turn(rx[first + 4 * top + i, 8:16, :], 2 * i, 0)
            out = tile if out is None else jnp.where(row == i, tile, out)
        halves.append(out)
    return jnp.concatenate(halves, axis=0)


def pack_columns(src, tx, group, extra=None):
    lane = lanes()
    rows = []
    for half in range(2):
        rows.append(
            [src[8 * half : 8 * half + 8, pl.ds(pl.multiple_of(group * 640 + 128 * t, 128), 128)] for t in range(5)]
        )

    def piece(tiles, start, to):
        t, o = start // 128, start % 128
        x = tiles[t]
        if o > 64:
            x = jnp.where(lane >= o, x, tiles[t + 1])
        return turn(x, to - o, 1)

    rests = []
    for half in range(2):
        out = None
        for i in range(8):
            t, o = (80 * i + 64) // 128, (80 * i + 64) % 128
            x = turn(rows[half][t], 16 * i - o, 1)
            out = x if out is None else jnp.where(lane // 16 == i, x, out)
        rests.append(out)
    swapped = swap_blocks(jnp.concatenate(rests, axis=0))
    for i in range(8):
        main = jnp.where(lane < 64, piece(rows[0], 80 * i, 0), piece(rows[1], 80 * i, 64))
        store_message(tx, group * 8 + i, main, swapped, i)
        if extra is not None:
            tx[group * 8 + i, MSG : MSG + 1, 0:ROWS] = extra[...]


def unpack_columns(rx, group):
    lane = lanes()
    rest = swap_blocks(load_swapped(rx, group * 8))
    out = [[None] * 5, [None] * 5]
    mains = [rx[group * 8 + i, 0:8, :] for i in range(8)]
    for half in range(2):
        part = rest[8 * half : 8 * half + 8]
        for t in range(5):
            x = jnp.zeros((8, 128), jnp.float32)
            for i in range(8):
                first = 80 * i - 128 * t
                if first + 64 > 0 and first < 128:
                    moved = turn(mains[i], first - 64 * half, 1)
                    x = jnp.where((lane >= first) & (lane < first + 64), moved, x)
                first = 80 * i + 64 - 128 * t
                if first >= 0 and first < 128:
                    moved = turn(part, first - 16 * i, 1)
                    x = jnp.where((lane >= first) & (lane < first + 16), moved, x)
            out[half][t] = x
    return [jnp.concatenate([out[0][t], out[1][t]], axis=0) for t in range(5)]


def unpack_rows(rx, group):
    lane = lanes()
    rest = swap_blocks(load_swapped(rx, group * 8))
    blocks = []
    for i in range(8):
        main = rx[group * 8 + i, 0:8, :]
        for half in range(2):
            part = turn(rest[8 * half : 8 * half + 8], 64 - 16 * i, 1)
            x = jnp.where(lane < 64, turn(main, 64 * half, 1), part)
            blocks.append(jnp.where(lane < 80, x, 0.0))
    return jnp.concatenate(blocks, axis=0)


def pack_rows(x, tx, group):
    lane = lanes()
    rests = []
    for half in range(2):
        out = None
        for i in range(8):
            part = turn(x[16 * i + 8 * half : 16 * i + 8 * half + 8], 16 * i - 64, 1)
            out = part if out is None else jnp.where(lane // 16 == i, part, out)
        rests.append(out)
    swapped = swap_blocks(jnp.concatenate(rests, axis=0))
    for i in range(8):
        main = jnp.where(lane < 64, x[16 * i : 16 * i + 8], turn(x[16 * i + 8 : 16 * i + 16], 64, 1))
        store_message(tx, group * 8 + i, main, swapped, i)


def halves_of(x):
    high = x.astype(jnp.bfloat16)
    return high, (x - high.astype(jnp.float32)).astype(jnp.bfloat16)


def column(ref, m):
    return ref[:, pl.ds(pl.multiple_of(m * 128, 128), 128)]


def kernel(
    p0, p1, tt, vt, rot, rw, cpl, cent, small_op, big_op,
    mid, last,
    tall, thigh, tlow, vs, pt, weighted, spread, acc, scaled, below, above, linear, link, stacked, radial, turned, couplings,
    scaled_points, below_points, above_points,
    tx0, tx1, tx2, tx3, rx0, rx1, rx2, rx3,
    own_sem, t_send, z_recv, y_recv, c_recv,
    a_send, a_recv, h_send, h_recv, g_send, g_recv, z_ready, c_ready,
):
    txs, rxs = (tx0, tx1, tx2, tx3), (rx0, rx1, rx2, rx3)
    y, z, c, h = [lax.axis_index(a) for a in GRID + ("hel",)]

    def slot(yy, zz, cc):
        return (yy * 4 + zz) * 2 + cc

    me = slot(y, z, c)
    up, down = (lax.rem(y + 1, 8), z, c, h), (lax.rem(y + 7, 8), z, c, h)
    twin = (y, z, 1 - c, h)
    y_line = [(lax.rem(y + i, 8), z, c, h) for i in range(1, 8)]
    z_line = [(y, lax.rem(z + i, 4), c, h) for i in range(1, 4)]
    higher, lower = (y, z, c, h + 1), (y, z, c, h - 1)

    barrier = pltpu.get_barrier_semaphore()
    for device in z_line + y_line + [twin]:
        pl.semaphore_signal(barrier, inc=1, device_id=device, device_id_type=MESH)

    @pl.when(h < 7)
    def _():
        pl.semaphore_signal(barrier, inc=1, device_id=higher, device_id_type=MESH)

    @pl.when(h > 0)
    def _():
        pl.semaphore_signal(barrier, inc=1, device_id=lower, device_id_type=MESH)

    own = pltpu.make_async_copy(tt, tall.at[me], own_sem)
    own.start()
    neighbours = 11 + (h > 0).astype(jnp.int32) + (h < 7).astype(jnp.int32)
    pl.semaphore_wait(barrier, neighbours)

    def hel_copies(up_src, up_dst, down_src, down_dst, send, recv):
        return (
            pltpu.make_async_remote_copy(
                src_ref=up_src, dst_ref=up_dst, send_sem=send(0), recv_sem=recv(0), device_id=higher, device_id_type=MESH
            ),
            pltpu.make_async_remote_copy(
                src_ref=down_src, dst_ref=down_dst, send_sem=send(1), recv_sem=recv(1), device_id=lower, device_id_type=MESH
            ),
        )

    def hel_first():
        return hel_copies(p1, below, scaled, above, lambda i: h_send.at[i], lambda i: h_recv.at[i])

    def hel_second(i, at):
        return hel_copies(
            spread.at[:, at], below_points.at[:, at], scaled_points.at[:, at], above_points.at[:, at],
            lambda way: g_send.at[i, way], lambda way: g_recv.at[i, way],
        )

    def hel_start(copies, ways=(0, 1)):
        if 0 in ways:

            @pl.when(h < 7)
            def _():
                copies()[0].start()

        if 1 in ways:

            @pl.when(h > 0)
            def _():
                copies()[1].start()

    def hel_wait(copies):
        @pl.when(h > 0)
        def _():
            copies()[0].wait_recv()

        @pl.when(h > 0)
        def _():
            copies()[1].wait_send()

        @pl.when(h < 7)
        def _():
            copies()[1].wait_recv()

        @pl.when(h < 7)
        def _():
            copies()[0].wait_send()

    def table_copy(place, part, recv, device, src=None):
        return pltpu.make_async_remote_copy(
            src_ref=(tall.at[place] if src is None else src).at[part], dst_ref=tall.at[place].at[part],
            send_sem=t_send, recv_sem=recv, device_id=device, device_id_type=MESH,
        )

    def arrived(recv, part):
        table_copy(0, part, recv, twin).wait_recv()

    REST = pl.ds(0, 24)

    def at_y(dy):
        return lax.rem(y + 8 + dy, 8)

    def rest_on(dy, zz, ahead, behind, src=None):
        place = slot(at_y(dy), zz, c)
        if ahead is not None:
            table_copy(place, REST, y_recv.at[0, ahead, zz], up, src).start()
        if behind is not None:
            table_copy(place, REST, y_recv.at[1, behind, zz], down, src).start()
        table_copy(place, REST, c_recv.at[dy % 8, zz], twin, src).start()

    def ring_rest(s):
        for i in range(4):
            zz = lax.rem(z + 4 - i, 4)
            on = s < 3 or (s == 3 and i < 2)
            if s < 4 or i < 2:
                arrived(y_recv.at[0, s - 1, zz], REST)
                rest_on(-s, zz, s if on else None, None)
            on = s < 3 or (s == 3 and i >= 2)
            if s < 4 or i >= 2:
                arrived(y_recv.at[1, s - 1, zz], REST)
                rest_on(s, zz, None, s if on else None)

    for i in range(1, 4):
        table_copy(me, REST, z_recv.at[i - 1], z_line[i - 1], tt).start()
    rest_on(0, z, 0, 0, tt)
    hel_start(hel_first, (0,))
    for device in z_line:
        pl.semaphore_signal(z_ready, inc=1, device_id=device, device_id_type=MESH)

    @pl.when(h == 0)
    def _():
        below[...] = jnp.zeros_like(below)
        below_points[...] = jnp.zeros_like(below_points)

    @pl.when(h == 7)
    def _():
        above[...] = jnp.zeros_like(above)
        above_points[...] = jnp.zeros_like(above_points)

    def exchange_start(k, group, dy):
        tx, rx = txs[k], rxs[k]
        rows = MSG + 1 if k == 0 else MSG

        @pl.loop(0, 8)
        def _(e):
            zz, cc = lax.rem(z + e // 2, 4), lax.rem(c + lax.rem(e, 2), 2)
            to = slot(group, zz, cc)
            itself = (dy == 0) & (e == 0)

            @pl.when(jnp.logical_not(itself))
            def _():
                pltpu.make_async_remote_copy(
                    src_ref=tx.at[to, pl.ds(0, rows)], dst_ref=rx.at[me, pl.ds(0, rows)],
                    send_sem=a_send.at[k], recv_sem=a_recv.at[k, lax.rem(8 - dy, 8)],
                    device_id=(group, zz, cc, h), device_id_type=MESH,
                ).start()

            @pl.when(itself)
            def _():
                rx[me] = tx[me]

    def far_first(i):
        return lax.rem(jnp.where(lax.rem(i, 2) == 1, 4 - (i + 1) // 2, 4 + i // 2), 8)

    def exchange_wait(k, dy):
        tx, rx = txs[k], rxs[k]
        rows = MSG + 1 if k == 0 else MSG

        def wait(count):
            pltpu.make_async_remote_copy(
                src_ref=tx.at[pl.ds(0, count), pl.ds(0, rows)], dst_ref=rx.at[pl.ds(0, count), pl.ds(0, rows)],
                send_sem=a_send.at[k], recv_sem=a_recv.at[k, dy], device_id=twin, device_id_type=MESH,
            ).wait_recv()

        @pl.when(dy == 0)
        def _():
            wait(7)

        @pl.when(dy != 0)
        def _():
            wait(8)

    def exchange_sent(k):
        rows = MSG + 1 if k == 0 else MSG
        pltpu.make_async_remote_copy(
            src_ref=txs[k].at[pl.ds(0, 63), pl.ds(0, rows)], dst_ref=rxs[k].at[pl.ds(0, 63), pl.ds(0, rows)],
            send_sem=a_send.at[k], recv_sem=a_recv.at[k, 0], device_id=twin, device_id_type=MESH,
        ).wait_send()

    def radial_big(src):
        for m in range(TILES):
            stacked[16 * m : 16 * m + 16] = src[:, 128 * m : 128 * m + 128]
        left = lanes((TILES, 128)) < 64

        @pl.loop(0, 2)
        def _(q):
            for r in range(4):
                j = 8 * q + 2 * r
                rows = [stacked[pl.ds(j + k, 48, stride=16), :] for k in range(2)]
                high, low = halves_of(jnp.concatenate(rows, axis=1))
                data = jnp.concatenate([high, low, high], axis=0)
                result = jnp.dot(big_op[...], data, preferred_element_type=jnp.float32)
                for k in range(2):
                    part = result[:, 128 * k : 128 * k + 128]
                    crossed = jnp.where(left, part[80:120], part[40:80])
                    radial[pl.ds(j + k, TILES, stride=16), :] = part[0:40] + turn(crossed, 64, 1)

    def local_part(src, older):
        @pl.loop(0, TILES // 8)
        def _(g):
            rows = stacked[pl.ds(pl.multiple_of(128 * g, 128), 128), :]
            high, low = halves_of(rows)
            small = jnp.dot(
                jnp.concatenate([high, low, high], axis=1), small_op[...], preferred_element_type=jnp.float32
            )
            whole = small + radial[pl.ds(pl.multiple_of(128 * g, 128), 128), :]
            for u in range(8):
                at = pl.ds(pl.multiple_of((8 * g + u) * 128, 128), 128)
                block = slice(16 * u, 16 * u + 16)
                linear[:, at] = FACTOR * (whole[block] + turned[...] * rows[block]) - older[:, at]

    def by_tiles(body):
        @pl.loop(0, TILES // 8)
        def _(g):
            for u in range(8):
                body(8 * g + u, pl.ds(pl.multiple_of((8 * g + u) * 128, 128), 128))

    def add_coriolis():
        def body(m, at):
            linear[:, at] = linear[:, at] + FACTOR * (link[:, at] * below[:, at] + above[:, at])

        by_tiles(body)

    def table_halves(yy):
        table = tall[pl.ds(yy * 8, 8)].reshape(192, J)
        high, low = halves_of(table)
        at = pl.ds(pl.multiple_of(yy * 192, 64), 192)
        thigh[at] = high
        tlow[at] = low

    nt = (((1,), (1,)), ((), ()))

    def points_of(at, potential):
        both = lax.dot_general(pt[...], thigh[at], nt, preferred_element_type=jnp.float32)
        cross = lax.dot_general(pt[0:NB], tlow[at], nt, preferred_element_type=jnp.float32)
        high, low = halves_of((both[0:NB] + both[NB:] + cross) * potential)
        return jnp.concatenate([high, low], axis=0)

    def back_of(points, high, low):
        both = jnp.dot(points, high, preferred_element_type=jnp.float32)
        cross = jnp.dot(points[0:NB], low, preferred_element_type=jnp.float32)
        return both[0:NB] + both[NB:] + cross

    def potential_part(yy, first):
        at = pl.ds(pl.multiple_of(yy * 192, 64), 192)
        total = back_of(points_of(at, vs[yy, :, 0:192]), thigh[at], tlow[at])
        if first:
            acc[0:NB] = total
        else:
            acc[0:NB] = acc[0:NB] + total

    diagonal = lax.broadcasted_iota(jnp.int32, (ROWS, ROWS), 0) == lanes((ROWS, ROWS))
    of_rows = lambda ref: jnp.sum(jnp.where(diagonal, ref[...], 0.0), axis=1, keepdims=True)
    lane = lanes((1, 128))
    centrifugal = cent[...]

    def pick(at):
        return jnp.sum(jnp.where(at == lanes((at.shape[0], RB)), centrifugal, 0.0), axis=1, keepdims=True)

    tile_at = lax.broadcasted_iota(jnp.int32, (TILES, 1), 0)
    of_tiles = jnp.where(lanes((TILES, 128)) < 64, pick(2 * tile_at), pick(2 * tile_at + 1))
    own_coupling = jnp.broadcast_to(of_rows(cpl), (ROWS, 128))
    for m in range(TILES):
        at = slice(128 * m, 128 * m + 128)
        factor = own_coupling * of_tiles[m : m + 1]
        link[:, at] = factor
        scaled[:, at] = factor * p1[:, at]
    hel_start(hel_first, (1,))

    @pl.loop(0, 8)
    def _(group):
        pack_columns(p1, tx0, group, cpl)


    pl.semaphore_wait(z_ready, 3)
    pl.semaphore_signal(c_ready, inc=1, device_id=twin, device_id_type=MESH)
    pl.semaphore_wait(c_ready, 1)

    @pl.loop(0, 8)
    def _(i):
        dy = far_first(i)
        exchange_start(0, lax.rem(y + dy, 8), dy)

    for i in range(1, 4):
        arrived(z_recv.at[i - 1], REST)
        rest_on(0, lax.rem(z + 4 - i, 4), 0, 0)

    weight = jnp.concatenate([rw[...], rw[...]], axis=1)
    turned[...] = of_rows(rot) * weight - centre
    stacked[640:768] = jnp.zeros((128, 128), jnp.float32)
    radial_big(p1)
    local_part(p1, p0)
    ring_rest(1)

    lane80 = lax.broadcasted_iota(jnp.int32, (NB, 128), 1)
    for yy in range(8):
        first = 192 * yy // 128
        a, b = vt[:, 128 * first : 128 * first + 128], vt[:, 128 * first + 128 : 128 * first + 256]
        if yy % 2:
            a, b = turn(a, 64, 1), turn(b, 64, 1)
            a = jnp.where(lane80 < 64, a, b)
        vs[yy, :, 0:128] = a
        vs[yy, :, 128:256] = b

    def compute(dy, first=False):
        for zz in range(4):
            arrived(c_recv.at[dy % 8, zz], REST)
        yy = at_y(dy)
        table_halves(yy)
        potential_part(yy, first)

    hel_wait(hel_first)
    add_coriolis()

    @pl.loop(0, 8)
    def _(i):
        dy = far_first(i)
        group = lax.rem(y + dy, 8)
        pack_columns(linear, tx1, group)
        exchange_start(1, group, dy)

    ring_rest(2)

    @pl.loop(0, 8)
    def _(dy):
        exchange_wait(0, dy)
        group = lax.rem(y + dy, 8)
        at = pl.ds(pl.multiple_of(group * 128, 128), 128)
        high, low = halves_of(unpack_rows(rx0, group).T[0:NB])
        pt[0:NB, at] = high
        pt[NB : 2 * NB, at] = low
        row = jnp.zeros((1, 128), jnp.float32)
        for i in range(8):
            part = turn(rx0[group * 8 + i, 8:16, :], 16 * i, 1)[2:3]
            row = jnp.where(lane // 16 == i, part, row)
        couplings[:, at] = row

    own.wait()
    compute(0, True)
    compute(1)
    compute(-1)
    ring_rest(3)
    compute(2)
    compute(-2)
    ring_rest(4)

    @pl.loop(0, 8)
    def _(dy):
        exchange_wait(1, dy)
        group = lax.rem(y + dy, 8)
        at = pl.ds(pl.multiple_of(group * 128, 128), 128)
        spread[:, at] = unpack_rows(rx1, group).T[0:NB]

    compute(3)
    compute(-3)
    compute(4)

    acc[NB:128] = jnp.zeros((128 - NB, J), jnp.float32)
    own_centrifugal = pick((me * NB + lax.broadcasted_iota(jnp.int32, (NB, 1), 0)) // RS)

    def pair_of(i):
        return lax.rem(y // 2 + jnp.where(i == 0, 2, jnp.where(i == 3, 0, 2 * i - 1)), 4)

    @pl.loop(0, 4)
    def _(i):
        at = pl.ds(pl.multiple_of(pair_of(i) * 256, 256), 256)
        packet = spread[:, at] + FACTOR * acc[0:NB, at]
        spread[:, at] = packet
        scaled_points[:, at] = own_centrifugal * couplings[:, at] * packet
        hel_start(lambda: hel_second(i, at))
        high, low = halves_of(packet)
        pt[0:NB, at] = high
        pt[NB : 2 * NB, at] = low

    @pl.loop(0, 8)
    def _(i):
        dy = far_first(i)
        group = lax.rem(y + dy, 8)
        pack_rows(acc[:, pl.ds(pl.multiple_of(group * 128, 128), 128)].T, tx2, group)
        exchange_start(2, group, dy)

    @pl.loop(0, 6)
    def _(i):
        at = pl.ds(pl.multiple_of(i * 256, 256), 256)
        weighted[:, at] = points_of(at, vt[:, at])

    @pl.loop(0, 4)
    def _(i):
        pair_at = pair_of(i)
        at = pl.ds(pl.multiple_of(pair_at * 256, 256), 256)
        total = back_of(weighted[...], thigh[:, at], tlow[:, at])
        hel_wait(lambda: hel_second(i, at))
        factor = own_centrifugal * couplings[:, at]
        acc[0:NB, at] = total + (factor * below_points[:, at] + above_points[:, at])
        for part in range(2):
            group = 2 * pair_at + part
            pack_rows(acc[:, pl.ds(pl.multiple_of(group * 128, 128), 128)].T, tx3, group)
            exchange_start(3, group, lax.rem(group - y + 8, 8))

    def take_back(k, out):
        @pl.loop(0, 8)
        def _(dy):
            exchange_wait(k, dy)
            group = lax.rem(y + dy, 8)
            for t, tile in enumerate(unpack_columns(rxs[k], group)):
                at = pl.ds(pl.multiple_of(group * 640 + 128 * t, 128), 128)
                out[:, at] = linear[:, at] + FACTOR * tile

    take_back(2, mid)
    radial_big(mid)
    local_part(mid, p1)
    take_back(3, last)

    for k in range(4):
        exchange_sent(k)
    pltpu.make_async_remote_copy(
        src_ref=tall.at[pl.ds(0, 63)], dst_ref=tall.at[pl.ds(0, 63)], send_sem=t_send, recv_sem=z_recv.at[0],
        device_id=twin, device_id_type=MESH,
    ).wait_send()


def hand_out(mid, last, mid_out, last_out):
    mid_out[...] = mid[...]
    last_out[...] = last[...]


def shards(packet_prev, packet_now, angular_table, potential, rotation, radial_weight, coupling, centrifugal):
    small_op, big_op = (jnp.asarray(a) for a in kinetic_tables())
    whole = jax.ShapeDtypeStruct((ROWS, TILES * 128), jnp.float32)
    vmem = pl.BlockSpec(memory_space=pltpu.VMEM)
    packet = (ROWS, TILES * 128)
    f32, bf16 = jnp.float32, jnp.bfloat16
    dma = pltpu.SemaphoreType.DMA
    mid, last = pl.pallas_call(
        kernel,
        out_shape=(whole, whole),
        in_specs=[vmem] * 10,
        out_specs=(vmem, vmem),
        scratch_shapes=[
            pltpu.VMEM((64, 24, J), f32),
            pltpu.VMEM((Q, J), bf16),
            pltpu.VMEM((Q, J), bf16),
            pltpu.VMEM((8, NB, 256), f32),
            pltpu.VMEM((2 * NB, J), bf16),
            pltpu.VMEM((2 * NB, Q), bf16),
            pltpu.VMEM((NB, J), f32),
            pltpu.VMEM((128, J), f32),
            *[pltpu.VMEM(packet, f32) for _ in range(5)],
            pltpu.VMEM((768, 128), f32),
            pltpu.VMEM((640, 128), f32),
            pltpu.VMEM((ROWS, 128), f32),
            pltpu.VMEM((1, J), f32),
            *[pltpu.VMEM((NB, J), f32) for _ in range(3)],
            *[pltpu.VMEM((64, 16, 128), f32) for _ in range(8)],
            dma,
            dma,
            dma((3,)),
            dma((2, 4, 4)),
            dma((8, 4)),
            dma((4,)),
            dma((4, 8)),
            dma((2,)),
            dma((2,)),
            dma((4, 2)),
            dma((4, 2)),
            pltpu.SemaphoreType.REGULAR,
            pltpu.SemaphoreType.REGULAR,
        ],
        compiler_params=pltpu.CompilerParams(collective_id=0, has_side_effects=True, vmem_limit_bytes=56 << 20),
        cost_estimate=pl.CostEstimate(flops=4 * 3 * 2 * J * Q * NB, bytes_accessed=4 << 20, transcendentals=0),
    )(
        packet_prev[0],
        packet_now[0],
        angular_table[0].T,
        potential.T,
        rotation,
        radial_weight.reshape(1, RS),
        coupling,
        centrifugal.reshape(1, RB),
        small_op,
        big_op,
    )
    mid, last = pl.pallas_call(
        hand_out, out_shape=(whole, whole), in_specs=[vmem] * 2, out_specs=(vmem, vmem)
    )(mid, last)
    return mid[None], last[None]


def solution(mesh):
    finer = Mesh(
        mesh.devices.reshape(8, 4, 2, mesh.shape["hel"]), ("grid_0", "grid_1", "grid_2", "hel")
    )
    placed = (
        P("hel", GRID, None),
        P("hel", GRID, None),
        P("hel", None, GRID),
        P(None, GRID),
        P("hel", GRID),
        P(),
        P("hel", GRID),
        P(),
    )
    return jax.shard_map(
        shards,
        mesh=finer,
        in_specs=placed,
        out_specs=(P("hel", GRID, None), P("hel", GRID, None)),
        check_vma=False,
    )
```

```python
import functools

import jax
import jax.numpy as jnp
import numpy as np
from jax import lax
from jax.experimental import pallas as pl
from jax.experimental.pallas import tpu as pltpu
from jax.sharding import Mesh
from jax.sharding import PartitionSpec as P

RB = 80
RS = 64
J = 1024
Q = 1536
NB = 80
ROWS = 16
TILES = 40
MSG = 10
GRID = ("grid_0", "grid_1", "grid_2")
MESH = pl.DeviceIdType.MESH

big_scale = 0.05
small_scale = 0.08
centre = 1.0
half_width = 1.5
FACTOR = 2.0 / half_width


def kinetic_entry(offset, coef):
    offset = np.asarray(offset, np.int64)
    parity = 1 - 2 * (np.abs(offset) % 2)
    square = np.maximum(offset * offset, 1)
    return (coef * np.where(offset == 0, np.pi**2 / 3.0, 2.0 * parity / square)).astype(np.float32)


def two_halves(x):
    high = x.astype(jnp.bfloat16)
    return high, (x - high.astype(np.float32)).astype(jnp.bfloat16)


def kinetic_tables():
    index = np.arange(RS)
    pair = np.zeros((128, 128), np.float32)
    pair[:64, :64] = pair[64:, 64:] = kinetic_entry(index[:, None] - index[None, :], small_scale)
    high, low = two_halves(pair)
    small = np.concatenate([high, high, low], axis=0)
    apart = 2 * (np.arange(TILES)[:, None] - np.arange(TILES)[None, :])
    big = np.zeros((128, 48), np.float32)
    for i, more in enumerate((0, -1, 1)):
        big[40 * i : 40 * i + 40, :40] = kinetic_entry(apart + more, big_scale)
    high, low = two_halves(big)
    return small, np.concatenate([high, high, low], axis=1)


def lanes(shape=(8, 128)):
    return lax.broadcasted_iota(jnp.int32, shape, 1)


def turn(x, shift, axis):
    shift = shift % x.shape[axis]
    return x if shift == 0 else pltpu.roll(x, shift, axis)


def swap_blocks(x):
    row = lax.broadcasted_iota(jnp.int32, (16, 128), 0) // 2
    lane = lanes((16, 128)) // 16
    apart = (row - lane + 8) % 8
    out = x
    for delta in range(1, 8):
        moved = turn(turn(x, 2 * delta, 0), -16 * delta, 1)
        out = jnp.where(apart == delta, moved, out)
    return out


def store_message(tx, place, main, swapped, i):
    tx[place, 0:8, :] = main
    half = swapped[0:8] if i < 4 else swapped[8:16]
    tx[place, 8:16, :] = turn(half, -2 * (i % 4), 0)


def load_swapped(rx, first):
    row = lax.broadcasted_iota(jnp.int32, (8, 128), 0) // 2
    halves = []
    for top in range(2):
        out = None
        for i in range(4):
            tile = turn(rx[first + 4 * top + i, 8:16, :], 2 * i, 0)
            out = tile if out is None else jnp.where(row == i, tile, out)
        halves.append(out)
    return jnp.concatenate(halves, axis=0)


def pack_columns(src, tx, group, extra=None):
    lane = lanes()
    rows = []
    for half in range(2):
        rows.append(
            [src[8 * half : 8 * half + 8, pl.ds(pl.multiple_of(group * 640 + 128 * t, 128), 128)] for t in range(5)]
        )

    def piece(tiles, start, to):
        t, o = start // 128, start % 128
        x = tiles[t]
        if o > 64:
            x = jnp.where(lane >= o, x, tiles[t + 1])
        return turn(x, to - o, 1)

    rests = []
    for half in range(2):
        out = None
        for i in range(8):
            t, o = (80 * i + 64) // 128, (80 * i + 64) % 128
            x = turn(rows[half][t], 16 * i - o, 1)
            out = x if out is None else jnp.where(lane // 16 == i, x, out)
        rests.append(out)
    swapped = swap_blocks(jnp.concatenate(rests, axis=0))
    for i in range(8):
        main = jnp.where(lane < 64, piece(rows[0], 80 * i, 0), piece(rows[1], 80 * i, 64))
        store_message(tx, group * 8 + i, main, swapped, i)
        if extra is not None:
            tx[group * 8 + i, MSG : MSG + 1, 0:ROWS] = extra[...]


def unpack_columns(rx, group):
    lane = lanes()
    rest = swap_blocks(load_swapped(rx, group * 8))
    out = [[None] * 5, [None] * 5]
    mains = [rx[group * 8 + i, 0:8, :] for i in range(8)]
    for half in range(2):
        part = rest[8 * half : 8 * half + 8]
        for t in range(5):
            x = jnp.zeros((8, 128), jnp.float32)
            for i in range(8):
                first = 80 * i - 128 * t
                if first + 64 > 0 and first < 128:
                    moved = turn(mains[i], first - 64 * half, 1)
                    x = jnp.where((lane >= first) & (lane < first + 64), moved, x)
                first = 80 * i + 64 - 128 * t
                if first >= 0 and first < 128:
                    moved = turn(part, first - 16 * i, 1)
                    x = jnp.where((lane >= first) & (lane < first + 16), moved, x)
            out[half][t] = x
    return [jnp.concatenate([out[0][t], out[1][t]], axis=0) for t in range(5)]


def unpack_rows(rx, group):
    lane = lanes()
    rest = swap_blocks(load_swapped(rx, group * 8))
    blocks = []
    for i in range(8):
        main = rx[group * 8 + i, 0:8, :]
        for half in range(2):
            part = turn(rest[8 * half : 8 * half + 8], 64 - 16 * i, 1)
            x = jnp.where(lane < 64, turn(main, 64 * half, 1), part)
            blocks.append(jnp.where(lane < 80, x, 0.0))
    return jnp.concatenate(blocks, axis=0)


def pack_rows(x, tx, group):
    lane = lanes()
    rests = []
    for half in range(2):
        out = None
        for i in range(8):
            part = turn(x[16 * i + 8 * half : 16 * i + 8 * half + 8], 16 * i - 64, 1)
            out = part if out is None else jnp.where(lane // 16 == i, part, out)
        rests.append(out)
    swapped = swap_blocks(jnp.concatenate(rests, axis=0))
    for i in range(8):
        main = jnp.where(lane < 64, x[16 * i : 16 * i + 8], turn(x[16 * i + 8 : 16 * i + 16], 64, 1))
        store_message(tx, group * 8 + i, main, swapped, i)


def halves_of(x):
    high = x.astype(jnp.bfloat16)
    return high, (x - high.astype(jnp.float32)).astype(jnp.bfloat16)


def column(ref, m):
    return ref[:, pl.ds(pl.multiple_of(m * 128, 128), 128)]


def kernel(
    p0, p1, tt, vt, rot, rw, cpl, cent, small_op, big_op,
    mid, last,
    tall, thigh, tlow, vs, pt, weighted, spread, acc, scaled, below, above, linear, link, stacked, radial, turned, couplings,
    scaled_points, below_points, above_points,
    tx0, tx1, tx2, tx3, rx0, rx1, rx2, rx3,
    own_sem, t_send, z_recv, y_recv, c_recv,
    a_send, a_recv, h_send, h_recv, g_send, g_recv, z_ready, c_ready,
):
    txs, rxs = (tx0, tx1, tx2, tx3), (rx0, rx1, rx2, rx3)
    y, z, c, h = [lax.axis_index(a) for a in GRID + ("hel",)]

    def slot(yy, zz, cc):
        return (yy * 4 + zz) * 2 + cc

    me = slot(y, z, c)
    up, down = (lax.rem(y + 1, 8), z, c, h), (lax.rem(y + 7, 8), z, c, h)
    twin = (y, z, 1 - c, h)
    y_line = [(lax.rem(y + i, 8), z, c, h) for i in range(1, 8)]
    z_line = [(y, lax.rem(z + i, 4), c, h) for i in range(1, 4)]
    higher, lower = (y, z, c, h + 1), (y, z, c, h - 1)

    barrier = pltpu.get_barrier_semaphore()
    for device in z_line + y_line + [twin]:
        pl.semaphore_signal(barrier, inc=1, device_id=device, device_id_type=MESH)

    @pl.when(h < 7)
    def _():
        pl.semaphore_signal(barrier, inc=1, device_id=higher, device_id_type=MESH)

    @pl.when(h > 0)
    def _():
        pl.semaphore_signal(barrier, inc=1, device_id=lower, device_id_type=MESH)

    own = pltpu.make_async_copy(tt, tall.at[me], own_sem)
    own.start()
    neighbours = 11 + (h > 0).astype(jnp.int32) + (h < 7).astype(jnp.int32)
    pl.semaphore_wait(barrier, neighbours)

    def hel_copies(up_src, up_dst, down_src, down_dst, send, recv):
        return (
            pltpu.make_async_remote_copy(
                src_ref=up_src, dst_ref=up_dst, send_sem=send(0), recv_sem=recv(0), device_id=higher, device_id_type=MESH
            ),
            pltpu.make_async_remote_copy(
                src_ref=down_src, dst_ref=down_dst, send_sem=send(1), recv_sem=recv(1), device_id=lower, device_id_type=MESH
            ),
        )

    def hel_first():
        return hel_copies(p1, below, scaled, above, lambda i: h_send.at[i], lambda i: h_recv.at[i])

    def hel_second(i, at):
        return hel_copies(
            spread.at[:, at], below_points.at[:, at], scaled_points.at[:, at], above_points.at[:, at],
            lambda way: g_send.at[i, way], lambda way: g_recv.at[i, way],
        )

    def hel_start(copies, ways=(0, 1)):
        if 0 in ways:

            @pl.when(h < 7)
            def _():
                copies()[0].start()

        if 1 in ways:

            @pl.when(h > 0)
            def _():
                copies()[1].start()

    def hel_wait(copies):
        @pl.when(h > 0)
        def _():
            copies()[0].wait_recv()

        @pl.when(h > 0)
        def _():
            copies()[1].wait_send()

        @pl.when(h < 7)
        def _():
            copies()[1].wait_recv()

        @pl.when(h < 7)
        def _():
            copies()[0].wait_send()

    def table_copy(place, part, recv, device, src=None):
        return pltpu.make_async_remote_copy(
            src_ref=(tall.at[place] if src is None else src).at[part], dst_ref=tall.at[place].at[part],
            send_sem=t_send, recv_sem=recv, device_id=device, device_id_type=MESH,
        )

    def arrived(recv, part):
        table_copy(0, part, recv, twin).wait_recv()

    REST = pl.ds(0, 24)

    def at_y(dy):
        return lax.rem(y + 8 + dy, 8)

    def rest_on(dy, zz, ahead, behind, src=None):
        place = slot(at_y(dy), zz, c)
        if ahead is not None:
            table_copy(place, REST, y_recv.at[0, ahead, zz], up, src).start()
        if behind is not None:
            table_copy(place, REST, y_recv.at[1, behind, zz], down, src).start()
        table_copy(place, REST, c_recv.at[dy % 8, zz], twin, src).start()

    def ring_rest(s):
        for i, far in enumerate((0, 1, 3, 2)):
            zz = lax.rem(z + 4 - far, 4)
            on = s < 3 or (s == 3 and i < 2)
            if s < 4 or i < 2:
                arrived(y_recv.at[0, s - 1, zz], REST)
                rest_on(-s, zz, s if on else None, None)
            on = s < 3 or (s == 3 and i >= 2)
            if s < 4 or i >= 2:
                arrived(y_recv.at[1, s - 1, zz], REST)
                rest_on(s, zz, None, s if on else None)

    for i in (1, 3, 2):
        table_copy(me, REST, z_recv.at[i - 1], z_line[i - 1], tt).start()
    rest_on(0, z, 0, 0, tt)
    hel_start(hel_first, (0,))
    for device in z_line:
        pl.semaphore_signal(z_ready, inc=1, device_id=device, device_id_type=MESH)

    @pl.when(h == 0)
    def _():
        below[...] = jnp.zeros_like(below)
        below_points[...] = jnp.zeros_like(below_points)

    @pl.when(h == 7)
    def _():
        above[...] = jnp.zeros_like(above)
        above_points[...] = jnp.zeros_like(above_points)

    def exchange_start(k, group, dy):
        tx, rx = txs[k], rxs[k]
        rows = MSG + 1 if k == 0 else MSG

        def send(e):
            zz, cc = lax.rem(z + e // 2, 4), (1 - c if e % 2 else c)
            to = slot(group, zz, cc)
            pltpu.make_async_remote_copy(
                src_ref=tx.at[to, pl.ds(0, rows)], dst_ref=rx.at[me, pl.ds(0, rows)],
                send_sem=a_send.at[k], recv_sem=a_recv.at[k, lax.rem(8 - dy, 8)],
                device_id=(group, zz, cc, h), device_id_type=MESH,
            ).start()

        for e in (4, 5, 2, 3, 6, 7, 1):
            send(e)

        @pl.when(dy != 0)
        def _():
            send(0)

        @pl.when(dy == 0)
        def _():
            rx[me] = tx[me]

    def far_first(i):
        return lax.rem(jnp.where(lax.rem(i, 2) == 1, 4 - (i + 1) // 2, 4 + i // 2), 8)

    def exchange_wait(k, dy):
        tx, rx = txs[k], rxs[k]
        rows = MSG + 1 if k == 0 else MSG

        def wait(count):
            pltpu.make_async_remote_copy(
                src_ref=tx.at[pl.ds(0, count), pl.ds(0, rows)], dst_ref=rx.at[pl.ds(0, count), pl.ds(0, rows)],
                send_sem=a_send.at[k], recv_sem=a_recv.at[k, dy], device_id=twin, device_id_type=MESH,
            ).wait_recv()

        @pl.when(dy == 0)
        def _():
            wait(7)

        @pl.when(dy != 0)
        def _():
            wait(8)

    def exchange_sent(k):
        rows = MSG + 1 if k == 0 else MSG
        pltpu.make_async_remote_copy(
            src_ref=txs[k].at[pl.ds(0, 63), pl.ds(0, rows)], dst_ref=rxs[k].at[pl.ds(0, 63), pl.ds(0, rows)],
            send_sem=a_send.at[k], recv_sem=a_recv.at[k, 0], device_id=twin, device_id_type=MESH,
        ).wait_send()

    def radial_big(src):
        for m in range(TILES):
            stacked[16 * m : 16 * m + 16] = src[:, 128 * m : 128 * m + 128]
        left = lanes((TILES, 128)) < 64

        @pl.loop(0, 2)
        def _(q):
            for r in range(4):
                j = 8 * q + 2 * r
                rows = [stacked[pl.ds(j + k, 48, stride=16), :] for k in range(2)]
                high, low = halves_of(jnp.concatenate(rows, axis=1))
                data = jnp.concatenate([high, low, high], axis=0)
                result = jnp.dot(big_op[...], data, preferred_element_type=jnp.float32)
                for k in range(2):
                    part = result[:, 128 * k : 128 * k + 128]
                    crossed = jnp.where(left, part[80:120], part[40:80])
                    radial[pl.ds(j + k, TILES, stride=16), :] = part[0:40] + turn(crossed, 64, 1)

    def local_part(src, older):
        @pl.loop(0, TILES // 8)
        def _(g):
            rows = stacked[pl.ds(pl.multiple_of(128 * g, 128), 128), :]
            high, low = halves_of(rows)
            small = jnp.dot(
                jnp.concatenate([high, low, high], axis=1), small_op[...], preferred_element_type=jnp.float32
            )
            whole = small + radial[pl.ds(pl.multiple_of(128 * g, 128), 128), :]
            for u in range(8):
                at = pl.ds(pl.multiple_of((8 * g + u) * 128, 128), 128)
                block = slice(16 * u, 16 * u + 16)
                linear[:, at] = FACTOR * (whole[block] + turned[...] * rows[block]) - older[:, at]

    def by_tiles(body):
        @pl.loop(0, TILES // 8)
        def _(g):
            for u in range(8):
                body(8 * g + u, pl.ds(pl.multiple_of((8 * g + u) * 128, 128), 128))

    def add_coriolis():
        def body(m, at):
            linear[:, at] = linear[:, at] + FACTOR * (link[:, at] * below[:, at] + above[:, at])

        by_tiles(body)

    def table_halves(yy):
        table = tall[pl.ds(yy * 8, 8)].reshape(192, J)
        high, low = halves_of(table)
        at = pl.ds(pl.multiple_of(yy * 192, 64), 192)
        thigh[at] = high
        tlow[at] = low

    nt = (((1,), (1,)), ((), ()))

    def points_of(at, potential):
        both = lax.dot_general(pt[...], thigh[at], nt, preferred_element_type=jnp.float32)
        cross = lax.dot_general(pt[0:NB], tlow[at], nt, preferred_element_type=jnp.float32)
        high, low = halves_of((both[0:NB] + both[NB:] + cross) * potential)
        return jnp.concatenate([high, low], axis=0)

    def back_of(points, high, low):
        both = jnp.dot(points, high, preferred_element_type=jnp.float32)
        cross = jnp.dot(points[0:NB], low, preferred_element_type=jnp.float32)
        return both[0:NB] + both[NB:] + cross

    def potential_part(yy, first):
        at = pl.ds(pl.multiple_of(yy * 192, 64), 192)
        total = back_of(points_of(at, vs[yy, :, 0:192]), thigh[at], tlow[at])
        if first:
            acc[0:NB] = total
        else:
            acc[0:NB] = acc[0:NB] + total

    diagonal = lax.broadcasted_iota(jnp.int32, (ROWS, ROWS), 0) == lanes((ROWS, ROWS))
    of_rows = lambda ref: jnp.sum(jnp.where(diagonal, ref[...], 0.0), axis=1, keepdims=True)
    lane = lanes((1, 128))
    centrifugal = cent[...]

    def pick(at):
        return jnp.sum(jnp.where(at == lanes((at.shape[0], RB)), centrifugal, 0.0), axis=1, keepdims=True)

    tile_at = lax.broadcasted_iota(jnp.int32, (TILES, 1), 0)
    of_tiles = jnp.where(lanes((TILES, 128)) < 64, pick(2 * tile_at), pick(2 * tile_at + 1))
    own_coupling = jnp.broadcast_to(of_rows(cpl), (ROWS, 128))
    for m in range(TILES):
        at = slice(128 * m, 128 * m + 128)
        factor = own_coupling * of_tiles[m : m + 1]
        link[:, at] = factor
        scaled[:, at] = factor * p1[:, at]
    hel_start(hel_first, (1,))

    @pl.loop(0, 8)
    def _(group):
        pack_columns(p1, tx0, group, cpl)


    def aside_on(i):
        arrived(z_recv.at[i - 1], REST)
        rest_on(0, lax.rem(z + 4 - i, 4), 0, 0)

    aside_on(1)
    aside_on(3)
    pl.semaphore_wait(z_ready, 3)
    pl.semaphore_signal(c_ready, inc=1, device_id=twin, device_id_type=MESH)
    pl.semaphore_wait(c_ready, 1)

    @pl.loop(0, 8)
    def _(i):
        dy = far_first(i)
        exchange_start(0, lax.rem(y + dy, 8), dy)

    aside_on(2)
    weight = jnp.concatenate([rw[...], rw[...]], axis=1)
    turned[...] = of_rows(rot) * weight - centre
    stacked[640:768] = jnp.zeros((128, 128), jnp.float32)
    radial_big(p1)
    local_part(p1, p0)
    ring_rest(1)

    lane80 = lax.broadcasted_iota(jnp.int32, (NB, 128), 1)
    for yy in range(8):
        first = 192 * yy // 128
        a, b = vt[:, 128 * first : 128 * first + 128], vt[:, 128 * first + 128 : 128 * first + 256]
        if yy % 2:
            a, b = turn(a, 64, 1), turn(b, 64, 1)
            a = jnp.where(lane80 < 64, a, b)
        vs[yy, :, 0:128] = a
        vs[yy, :, 128:256] = b

    def compute(dy, first=False):
        for zz in range(4):
            arrived(c_recv.at[dy % 8, zz], REST)
        yy = at_y(dy)
        table_halves(yy)
        potential_part(yy, first)

    hel_wait(hel_first)
    add_coriolis()

    @pl.loop(0, 8)
    def _(i):
        dy = far_first(i)
        group = lax.rem(y + dy, 8)
        pack_columns(linear, tx1, group)
        exchange_start(1, group, dy)

    ring_rest(2)

    @pl.loop(0, 8)
    def _(dy):
        exchange_wait(0, dy)
        group = lax.rem(y + dy, 8)
        at = pl.ds(pl.multiple_of(group * 128, 128), 128)
        high, low = halves_of(unpack_rows(rx0, group).T[0:NB])
        pt[0:NB, at] = high
        pt[NB : 2 * NB, at] = low
        row = jnp.zeros((1, 128), jnp.float32)
        for i in range(8):
            part = turn(rx0[group * 8 + i, 8:16, :], 16 * i, 1)[2:3]
            row = jnp.where(lane // 16 == i, part, row)
        couplings[:, at] = row

    own.wait()
    compute(0, True)
    compute(1)
    compute(-1)
    ring_rest(3)
    compute(2)
    compute(-2)

    @pl.loop(0, 8)
    def _(dy):
        exchange_wait(1, dy)
        group = lax.rem(y + dy, 8)
        at = pl.ds(pl.multiple_of(group * 128, 128), 128)
        spread[:, at] = unpack_rows(rx1, group).T[0:NB]

    compute(3)
    compute(-3)
    ring_rest(4)
    compute(4)

    acc[NB:128] = jnp.zeros((128 - NB, J), jnp.float32)
    own_centrifugal = pick((me * NB + lax.broadcasted_iota(jnp.int32, (NB, 1), 0)) // RS)

    def pair_of(i):
        return lax.rem(y // 2 + jnp.where(i == 0, 2, jnp.where(i == 3, 0, 2 * i - 1)), 4)

    @pl.loop(0, 4)
    def _(i):
        at = pl.ds(pl.multiple_of(pair_of(i) * 256, 256), 256)
        packet = spread[:, at] + FACTOR * acc[0:NB, at]
        spread[:, at] = packet
        scaled_points[:, at] = own_centrifugal * couplings[:, at] * packet
        hel_start(lambda: hel_second(i, at))
        high, low = halves_of(packet)
        pt[0:NB, at] = high
        pt[NB : 2 * NB, at] = low

    @pl.loop(0, 8)
    def _(i):
        dy = far_first(i)
        group = lax.rem(y + dy, 8)
        pack_rows(acc[:, pl.ds(pl.multiple_of(group * 128, 128), 128)].T, tx2, group)
        exchange_start(2, group, dy)

    @pl.loop(0, 6)
    def _(i):
        at = pl.ds(pl.multiple_of(i * 256, 256), 256)
        weighted[:, at] = points_of(at, vt[:, at])

    @pl.loop(0, 4)
    def _(i):
        pair_at = pair_of(i)
        at = pl.ds(pl.multiple_of(pair_at * 256, 256), 256)
        total = back_of(weighted[...], thigh[:, at], tlow[:, at])
        hel_wait(lambda: hel_second(i, at))
        factor = own_centrifugal * couplings[:, at]
        acc[0:NB, at] = total + (factor * below_points[:, at] + above_points[:, at])
        for part in range(2):
            group = 2 * pair_at + part
            pack_rows(acc[:, pl.ds(pl.multiple_of(group * 128, 128), 128)].T, tx3, group)
            exchange_start(3, group, lax.rem(group - y + 8, 8))

    def take_back(k, out):
        @pl.loop(0, 8)
        def _(dy):
            exchange_wait(k, dy)
            group = lax.rem(y + dy, 8)
            for t, tile in enumerate(unpack_columns(rxs[k], group)):
                at = pl.ds(pl.multiple_of(group * 640 + 128 * t, 128), 128)
                out[:, at] = linear[:, at] + FACTOR * tile

    take_back(2, mid)
    radial_big(mid)
    local_part(mid, p1)
    take_back(3, last)

    for k in range(4):
        exchange_sent(k)
    pltpu.make_async_remote_copy(
        src_ref=tall.at[pl.ds(0, 63)], dst_ref=tall.at[pl.ds(0, 63)], send_sem=t_send, recv_sem=z_recv.at[0],
        device_id=twin, device_id_type=MESH,
    ).wait_send()


def hand_out(mid, last, mid_out, last_out):
    mid_out[...] = mid[...]
    last_out[...] = last[...]


def shards(packet_prev, packet_now, angular_table, potential, rotation, radial_weight, coupling, centrifugal):
    small_op, big_op = (jnp.asarray(a) for a in kinetic_tables())
    whole = jax.ShapeDtypeStruct((ROWS, TILES * 128), jnp.float32)
    vmem = pl.BlockSpec(memory_space=pltpu.VMEM)
    packet = (ROWS, TILES * 128)
    f32, bf16 = jnp.float32, jnp.bfloat16
    dma = pltpu.SemaphoreType.DMA
    mid, last = pl.pallas_call(
        kernel,
        out_shape=(whole, whole),
        in_specs=[vmem] * 10,
        out_specs=(vmem, vmem),
        scratch_shapes=[
            pltpu.VMEM((64, 24, J), f32),
            pltpu.VMEM((Q, J), bf16),
            pltpu.VMEM((Q, J), bf16),
            pltpu.VMEM((8, NB, 256), f32),
            pltpu.VMEM((2 * NB, J), bf16),
            pltpu.VMEM((2 * NB, Q), bf16),
            pltpu.VMEM((NB, J), f32),
            pltpu.VMEM((128, J), f32),
            *[pltpu.VMEM(packet, f32) for _ in range(5)],
            pltpu.VMEM((768, 128), f32),
            pltpu.VMEM((640, 128), f32),
            pltpu.VMEM((ROWS, 128), f32),
            pltpu.VMEM((1, J), f32),
            *[pltpu.VMEM((NB, J), f32) for _ in range(3)],
            *[pltpu.VMEM((64, 16, 128), f32) for _ in range(8)],
            dma,
            dma,
            dma((3,)),
            dma((2, 4, 4)),
            dma((8, 4)),
            dma((4,)),
            dma((4, 8)),
            dma((2,)),
            dma((2,)),
            dma((4, 2)),
            dma((4, 2)),
            pltpu.SemaphoreType.REGULAR,
            pltpu.SemaphoreType.REGULAR,
        ],
        compiler_params=pltpu.CompilerParams(collective_id=0, has_side_effects=True, vmem_limit_bytes=56 << 20),
        cost_estimate=pl.CostEstimate(flops=4 * 3 * 2 * J * Q * NB, bytes_accessed=4 << 20, transcendentals=0),
    )(
        packet_prev[0],
        packet_now[0],
        angular_table[0].T,
        potential.T,
        rotation,
        radial_weight.reshape(1, RS),
        coupling,
        centrifugal.reshape(1, RB),
        small_op,
        big_op,
    )
    mid, last = pl.pallas_call(
        hand_out, out_shape=(whole, whole), in_specs=[vmem] * 2, out_specs=(vmem, vmem)
    )(mid, last)
    return mid[None], last[None]


def solution(mesh):
    finer = Mesh(
        mesh.devices.reshape(8, 4, 2, mesh.shape["hel"]), ("grid_0", "grid_1", "grid_2", "hel")
    )
    placed = (
        P("hel", GRID, None),
        P("hel", GRID, None),
        P("hel", None, GRID),
        P(None, GRID),
        P("hel", GRID),
        P(),
        P("hel", GRID),
        P(),
    )
    return jax.shard_map(
        shards,
        mesh=finer,
        in_specs=placed,
        out_specs=(P("hel", GRID, None), P("hel", GRID, None)),
        check_vma=False,
    )
```

```python
import functools

import jax
import jax.numpy as jnp
import numpy as np
from jax import lax
from jax.experimental import pallas as pl
from jax.experimental.pallas import tpu as pltpu
from jax.sharding import Mesh
from jax.sharding import PartitionSpec as P

RB = 80
RS = 64
J = 1024
Q = 1536
NB = 80
ROWS = 16
TILES = 40
MSG = 10
GRID = ("grid_0", "grid_1", "grid_2")
MESH = pl.DeviceIdType.MESH

big_scale = 0.05
small_scale = 0.08
centre = 1.0
half_width = 1.5
FACTOR = 2.0 / half_width


def kinetic_entry(offset, coef):
    offset = np.asarray(offset, np.int64)
    parity = 1 - 2 * (np.abs(offset) % 2)
    square = np.maximum(offset * offset, 1)
    return (coef * np.where(offset == 0, np.pi**2 / 3.0, 2.0 * parity / square)).astype(np.float32)


def two_halves(x):
    high = x.astype(jnp.bfloat16)
    return high, (x - high.astype(np.float32)).astype(jnp.bfloat16)


def kinetic_tables():
    index = np.arange(RS)
    pair = np.zeros((128, 128), np.float32)
    pair[:64, :64] = pair[64:, 64:] = kinetic_entry(index[:, None] - index[None, :], small_scale)
    high, low = two_halves(pair)
    small = np.concatenate([high, high, low], axis=0)
    apart = 2 * (np.arange(TILES)[:, None] - np.arange(TILES)[None, :])
    big = np.zeros((128, 48), np.float32)
    for i, more in enumerate((0, -1, 1)):
        big[40 * i : 40 * i + 40, :40] = kinetic_entry(apart + more, big_scale)
    high, low = two_halves(big)
    return small, np.concatenate([high, high, low], axis=1)


def lanes(shape=(8, 128)):
    return lax.broadcasted_iota(jnp.int32, shape, 1)


def turn(x, shift, axis):
    shift = shift % x.shape[axis]
    return x if shift == 0 else pltpu.roll(x, shift, axis)


def swap_blocks(x):
    row = lax.broadcasted_iota(jnp.int32, (16, 128), 0) // 2
    lane = lanes((16, 128)) // 16
    apart = (row - lane + 8) % 8
    out = x
    for delta in range(1, 8):
        moved = turn(turn(x, 2 * delta, 0), -16 * delta, 1)
        out = jnp.where(apart == delta, moved, out)
    return out


def store_message(tx, place, main, swapped, i):
    tx[place, 0:8, :] = main
    half = swapped[0:8] if i < 4 else swapped[8:16]
    tx[place, 8:16, :] = turn(half, -2 * (i % 4), 0)


def load_swapped(rx, first):
    row = lax.broadcasted_iota(jnp.int32, (8, 128), 0) // 2
    halves = []
    for top in range(2):
        out = None
        for i in range(4):
            tile = turn(rx[first + 4 * top + i, 8:16, :], 2 * i, 0)
            out = tile if out is None else jnp.where(row == i, tile, out)
        halves.append(out)
    return jnp.concatenate(halves, axis=0)


def pack_columns(src, tx, group, extra=None):
    lane = lanes()
    rows = []
    for half in range(2):
        rows.append(
            [src[8 * half : 8 * half + 8, pl.ds(pl.multiple_of(group * 640 + 128 * t, 128), 128)] for t in range(5)]
        )

    def piece(tiles, start, to):
        t, o = start // 128, start % 128
        x = tiles[t]
        if o > 64:
            x = jnp.where(lane >= o, x, tiles[t + 1])
        return turn(x, to - o, 1)

    rests = []
    for half in range(2):
        out = None
        for i in range(8):
            t, o = (80 * i + 64) // 128, (80 * i + 64) % 128
            x = turn(rows[half][t], 16 * i - o, 1)
            out = x if out is None else jnp.where(lane // 16 == i, x, out)
        rests.append(out)
    swapped = swap_blocks(jnp.concatenate(rests, axis=0))
    for i in range(8):
        main = jnp.where(lane < 64, piece(rows[0], 80 * i, 0), piece(rows[1], 80 * i, 64))
        store_message(tx, group * 8 + i, main, swapped, i)
        if extra is not None:
            tx[group * 8 + i, MSG : MSG + 1, 0:ROWS] = extra[...]


def unpack_columns(rx, group):
    lane = lanes()
    rest = swap_blocks(load_swapped(rx, group * 8))
    out = [[None] * 5, [None] * 5]
    mains = [rx[group * 8 + i, 0:8, :] for i in range(8)]
    for half in range(2):
        part = rest[8 * half : 8 * half + 8]
        for t in range(5):
            x = jnp.zeros((8, 128), jnp.float32)
            for i in range(8):
                first = 80 * i - 128 * t
                if first + 64 > 0 and first < 128:
                    moved = turn(mains[i], first - 64 * half, 1)
                    x = jnp.where((lane >= first) & (lane < first + 64), moved, x)
                first = 80 * i + 64 - 128 * t
                if first >= 0 and first < 128:
                    moved = turn(part, first - 16 * i, 1)
                    x = jnp.where((lane >= first) & (lane < first + 16), moved, x)
            out[half][t] = x
    return [jnp.concatenate([out[0][t], out[1][t]], axis=0) for t in range(5)]


def unpack_rows(rx, group):
    lane = lanes()
    rest = swap_blocks(load_swapped(rx, group * 8))
    blocks = []
    for i in range(8):
        main = rx[group * 8 + i, 0:8, :]
        for half in range(2):
            part = turn(rest[8 * half : 8 * half + 8], 64 - 16 * i, 1)
            x = jnp.where(lane < 64, turn(main, 64 * half, 1), part)
            blocks.append(jnp.where(lane < 80, x, 0.0))
    return jnp.concatenate(blocks, axis=0)


def pack_rows(x, tx, group):
    lane = lanes()
    rests = []
    for half in range(2):
        out = None
        for i in range(8):
            part = turn(x[16 * i + 8 * half : 16 * i + 8 * half + 8], 16 * i - 64, 1)
            out = part if out is None else jnp.where(lane // 16 == i, part, out)
        rests.append(out)
    swapped = swap_blocks(jnp.concatenate(rests, axis=0))
    for i in range(8):
        main = jnp.where(lane < 64, x[16 * i : 16 * i + 8], turn(x[16 * i + 8 : 16 * i + 16], 64, 1))
        store_message(tx, group * 8 + i, main, swapped, i)


def halves_of(x):
    high = x.astype(jnp.bfloat16)
    return high, (x - high.astype(jnp.float32)).astype(jnp.bfloat16)


def column(ref, m):
    return ref[:, pl.ds(pl.multiple_of(m * 128, 128), 128)]


def kernel(
    p0, p1, tt, vt, rot, rw, cpl, cent, small_op, big_op,
    mid, last,
    tall, thigh, tlow, vs, pt, weighted, spread, acc, scaled, below, above, linear, link, stacked, radial, turned, couplings,
    scaled_points, below_points, above_points,
    tx0, tx1, tx2, tx3, rx0, rx1, rx2, rx3,
    own_sem, t_send, z_recv, y_recv, c_recv,
    a_send, a_recv, h_send, h_recv, g_send, g_recv, z_ready, c_ready,
):
    txs, rxs = (tx0, tx1, tx2, tx3), (rx0, rx1, rx2, rx3)
    y, z, c, h = [lax.axis_index(a) for a in GRID + ("hel",)]

    def slot(yy, zz, cc):
        return (yy * 4 + zz) * 2 + cc

    me = slot(y, z, c)
    up, down = (lax.rem(y + 1, 8), z, c, h), (lax.rem(y + 7, 8), z, c, h)
    twin = (y, z, 1 - c, h)
    y_line = [(lax.rem(y + i, 8), z, c, h) for i in range(1, 8)]
    z_line = [(y, lax.rem(z + i, 4), c, h) for i in range(1, 4)]
    higher, lower = (y, z, c, h + 1), (y, z, c, h - 1)

    barrier = pltpu.get_barrier_semaphore()
    for device in z_line + y_line + [twin]:
        pl.semaphore_signal(barrier, inc=1, device_id=device, device_id_type=MESH)

    @pl.when(h < 7)
    def _():
        pl.semaphore_signal(barrier, inc=1, device_id=higher, device_id_type=MESH)

    @pl.when(h > 0)
    def _():
        pl.semaphore_signal(barrier, inc=1, device_id=lower, device_id_type=MESH)

    own = pltpu.make_async_copy(tt, tall.at[me], own_sem)
    own.start()
    neighbours = 11 + (h > 0).astype(jnp.int32) + (h < 7).astype(jnp.int32)
    pl.semaphore_wait(barrier, neighbours)

    def hel_copies(up_src, up_dst, down_src, down_dst, send, recv):
        return (
            pltpu.make_async_remote_copy(
                src_ref=up_src, dst_ref=up_dst, send_sem=send(0), recv_sem=recv(0), device_id=higher, device_id_type=MESH
            ),
            pltpu.make_async_remote_copy(
                src_ref=down_src, dst_ref=down_dst, send_sem=send(1), recv_sem=recv(1), device_id=lower, device_id_type=MESH
            ),
        )

    def hel_first():
        return hel_copies(p1, below, scaled, above, lambda i: h_send.at[i], lambda i: h_recv.at[i])

    def hel_second(i, at):
        return hel_copies(
            spread.at[:, at], below_points.at[:, at], scaled_points.at[:, at], above_points.at[:, at],
            lambda way: g_send.at[i, way], lambda way: g_recv.at[i, way],
        )

    def hel_start(copies, ways=(0, 1)):
        if 0 in ways:

            @pl.when(h < 7)
            def _():
                copies()[0].start()

        if 1 in ways:

            @pl.when(h > 0)
            def _():
                copies()[1].start()

    def hel_wait(copies):
        @pl.when(h > 0)
        def _():
            copies()[0].wait_recv()

        @pl.when(h > 0)
        def _():
            copies()[1].wait_send()

        @pl.when(h < 7)
        def _():
            copies()[1].wait_recv()

        @pl.when(h < 7)
        def _():
            copies()[0].wait_send()

    def table_copy(place, part, recv, device, src=None):
        return pltpu.make_async_remote_copy(
            src_ref=(tall.at[place] if src is None else src).at[part], dst_ref=tall.at[place].at[part],
            send_sem=t_send, recv_sem=recv, device_id=device, device_id_type=MESH,
        )

    def arrived(recv, part):
        table_copy(0, part, recv, twin).wait_recv()

    REST = pl.ds(0, 24)

    def at_y(dy):
        return lax.rem(y + 8 + dy, 8)

    def rest_on(dy, zz, ahead, behind, src=None):
        place = slot(at_y(dy), zz, c)
        if ahead is not None:
            table_copy(place, REST, y_recv.at[0, ahead, zz], up, src).start()
        if behind is not None:
            table_copy(place, REST, y_recv.at[1, behind, zz], down, src).start()
        table_copy(place, REST, c_recv.at[dy % 8, zz], twin, src).start()

    def ring_rest(s):
        for i, far in enumerate((0, 1, 3, 2)):
            zz = lax.rem(z + 4 - far, 4)
            on = s < 3 or (s == 3 and i < 2)
            if s < 4 or i < 2:
                arrived(y_recv.at[0, s - 1, zz], REST)
                rest_on(-s, zz, s if on else None, None)
            on = s < 3 or (s == 3 and i >= 2)
            if s < 4 or i >= 2:
                arrived(y_recv.at[1, s - 1, zz], REST)
                rest_on(s, zz, None, s if on else None)

    for i in (1, 3, 2):
        table_copy(me, REST, z_recv.at[i - 1], z_line[i - 1], tt).start()
    rest_on(0, z, 0, 0, tt)
    hel_start(hel_first, (0,))
    for device in z_line:
        pl.semaphore_signal(z_ready, inc=1, device_id=device, device_id_type=MESH)

    @pl.when(h == 0)
    def _():
        below[...] = jnp.zeros_like(below)
        below_points[...] = jnp.zeros_like(below_points)

    @pl.when(h == 7)
    def _():
        above[...] = jnp.zeros_like(above)
        above_points[...] = jnp.zeros_like(above_points)

    def exchange_start(k, group, dy):
        tx, rx = txs[k], rxs[k]
        rows = MSG + 1 if k == 0 else MSG

        def send(e):
            zz, cc = lax.rem(z + e // 2, 4), (1 - c if e % 2 else c)
            to = slot(group, zz, cc)
            pltpu.make_async_remote_copy(
                src_ref=tx.at[to, pl.ds(0, rows)], dst_ref=rx.at[me, pl.ds(0, rows)],
                send_sem=a_send.at[k], recv_sem=a_recv.at[k, lax.rem(8 - dy, 8)],
                device_id=(group, zz, cc, h), device_id_type=MESH,
            ).start()

        for e in (4, 5, 2, 3, 6, 7, 1):
            send(e)

        @pl.when(dy != 0)
        def _():
            send(0)

        @pl.when(dy == 0)
        def _():
            rx[me] = tx[me]

    def far_first(i):
        return lax.rem(jnp.where(lax.rem(i, 2) == 1, 4 - (i + 1) // 2, 4 + i // 2), 8)

    def exchange_wait(k, dy):
        tx, rx = txs[k], rxs[k]
        rows = MSG + 1 if k == 0 else MSG

        def wait(count):
            pltpu.make_async_remote_copy(
                src_ref=tx.at[pl.ds(0, count), pl.ds(0, rows)], dst_ref=rx.at[pl.ds(0, count), pl.ds(0, rows)],
                send_sem=a_send.at[k], recv_sem=a_recv.at[k, dy], device_id=twin, device_id_type=MESH,
            ).wait_recv()

        @pl.when(dy == 0)
        def _():
            wait(7)

        @pl.when(dy != 0)
        def _():
            wait(8)

    def exchange_sent(k):
        rows = MSG + 1 if k == 0 else MSG
        pltpu.make_async_remote_copy(
            src_ref=txs[k].at[pl.ds(0, 63), pl.ds(0, rows)], dst_ref=rxs[k].at[pl.ds(0, 63), pl.ds(0, rows)],
            send_sem=a_send.at[k], recv_sem=a_recv.at[k, 0], device_id=twin, device_id_type=MESH,
        ).wait_send()

    def radial_big(src):
        for m in range(TILES):
            stacked[16 * m : 16 * m + 16] = src[:, 128 * m : 128 * m + 128]
        left = lanes((TILES, 128)) < 64

        @pl.loop(0, 2)
        def _(q):
            for r in range(4):
                j = 8 * q + 2 * r
                rows = [stacked[pl.ds(j + k, 48, stride=16), :] for k in range(2)]
                high, low = halves_of(jnp.concatenate(rows, axis=1))
                data = jnp.concatenate([high, low, high], axis=0)
                result = jnp.dot(big_op[...], data, preferred_element_type=jnp.float32)
                for k in range(2):
                    part = result[:, 128 * k : 128 * k + 128]
                    crossed = jnp.where(left, part[80:120], part[40:80])
                    radial[pl.ds(j + k, TILES, stride=16), :] = part[0:40] + turn(crossed, 64, 1)

    def local_part(src, older):
        @pl.loop(0, TILES // 8)
        def _(g):
            rows = stacked[pl.ds(pl.multiple_of(128 * g, 128), 128), :]
            high, low = halves_of(rows)
            small = jnp.dot(
                jnp.concatenate([high, low, high], axis=1), small_op[...], preferred_element_type=jnp.float32
            )
            whole = small + radial[pl.ds(pl.multiple_of(128 * g, 128), 128), :]
            for u in range(8):
                at = pl.ds(pl.multiple_of((8 * g + u) * 128, 128), 128)
                block = slice(16 * u, 16 * u + 16)
                linear[:, at] = FACTOR * (whole[block] + turned[...] * rows[block]) - older[:, at]

    def by_tiles(body):
        @pl.loop(0, TILES // 8)
        def _(g):
            for u in range(8):
                body(8 * g + u, pl.ds(pl.multiple_of((8 * g + u) * 128, 128), 128))

    def add_coriolis():
        def body(m, at):
            linear[:, at] = linear[:, at] + FACTOR * (link[:, at] * below[:, at] + above[:, at])

        by_tiles(body)

    def table_halves(yy):
        table = tall[pl.ds(yy * 8, 8)].reshape(192, J)
        high, low = halves_of(table)
        at = pl.ds(pl.multiple_of(yy * 192, 64), 192)
        thigh[at] = high
        tlow[at] = low

    nt = (((1,), (1,)), ((), ()))

    def points_of(at, potential):
        both = lax.dot_general(pt[...], thigh[at], nt, preferred_element_type=jnp.float32)
        cross = lax.dot_general(pt[0:NB], tlow[at], nt, preferred_element_type=jnp.float32)
        high, low = halves_of((both[0:NB] + both[NB:] + cross) * potential)
        return jnp.concatenate([high, low], axis=0)

    def back_of(points, high, low):
        both = jnp.dot(points, high, preferred_element_type=jnp.float32)
        cross = jnp.dot(points[0:NB], low, preferred_element_type=jnp.float32)
        return both[0:NB] + both[NB:] + cross

    def potential_part(yy, first):
        at = pl.ds(pl.multiple_of(yy * 192, 64), 192)
        total = back_of(points_of(at, vs[yy, :, 0:192]), thigh[at], tlow[at])
        if first:
            acc[0:NB] = total
        else:
            acc[0:NB] = acc[0:NB] + total

    diagonal = lax.broadcasted_iota(jnp.int32, (ROWS, ROWS), 0) == lanes((ROWS, ROWS))
    of_rows = lambda ref: jnp.sum(jnp.where(diagonal, ref[...], 0.0), axis=1, keepdims=True)
    lane = lanes((1, 128))
    centrifugal = cent[...]

    def pick(at):
        return jnp.sum(jnp.where(at == lanes((at.shape[0], RB)), centrifugal, 0.0), axis=1, keepdims=True)

    tile_at = lax.broadcasted_iota(jnp.int32, (TILES, 1), 0)
    of_tiles = jnp.where(lanes((TILES, 128)) < 64, pick(2 * tile_at), pick(2 * tile_at + 1))
    own_coupling = jnp.broadcast_to(of_rows(cpl), (ROWS, 128))
    for m in range(TILES):
        at = slice(128 * m, 128 * m + 128)
        factor = own_coupling * of_tiles[m : m + 1]
        link[:, at] = factor
        scaled[:, at] = factor * p1[:, at]
    hel_start(hel_first, (1,))

    @pl.loop(0, 8)
    def _(group):
        pack_columns(p1, tx0, group, cpl)


    def aside_on(i):
        arrived(z_recv.at[i - 1], REST)
        rest_on(0, lax.rem(z + 4 - i, 4), 0, 0)

    aside_on(1)
    aside_on(3)
    pl.semaphore_wait(z_ready, 3)
    pl.semaphore_signal(c_ready, inc=1, device_id=twin, device_id_type=MESH)
    pl.semaphore_wait(c_ready, 1)

    @pl.loop(0, 8)
    def _(i):
        dy = far_first(i)
        exchange_start(0, lax.rem(y + dy, 8), dy)

    aside_on(2)
    weight = jnp.concatenate([rw[...], rw[...]], axis=1)
    turned[...] = of_rows(rot) * weight - centre
    stacked[640:768] = jnp.zeros((128, 128), jnp.float32)
    radial_big(p1)
    local_part(p1, p0)
    ring_rest(1)

    lane80 = lax.broadcasted_iota(jnp.int32, (NB, 128), 1)
    for yy in range(8):
        first = 192 * yy // 128
        a, b = vt[:, 128 * first : 128 * first + 128], vt[:, 128 * first + 128 : 128 * first + 256]
        if yy % 2:
            a, b = turn(a, 64, 1), turn(b, 64, 1)
            a = jnp.where(lane80 < 64, a, b)
        vs[yy, :, 0:128] = a
        vs[yy, :, 128:256] = b

    def compute(dy, first=False):
        for zz in range(4):
            arrived(c_recv.at[dy % 8, zz], REST)
        yy = at_y(dy)
        table_halves(yy)
        potential_part(yy, first)

    hel_wait(hel_first)
    add_coriolis()

    @pl.loop(0, 8)
    def _(i):
        dy = far_first(i)
        group = lax.rem(y + dy, 8)
        pack_columns(linear, tx1, group)
        exchange_start(1, group, dy)

    ring_rest(2)

    @pl.loop(0, 8)
    def _(dy):
        exchange_wait(0, dy)
        group = lax.rem(y + dy, 8)
        at = pl.ds(pl.multiple_of(group * 128, 128), 128)
        high, low = halves_of(unpack_rows(rx0, group).T[0:NB])
        pt[0:NB, at] = high
        pt[NB : 2 * NB, at] = low
        row = jnp.zeros((1, 128), jnp.float32)
        for i in range(8):
            part = turn(rx0[group * 8 + i, 8:16, :], 16 * i, 1)[2:3]
            row = jnp.where(lane // 16 == i, part, row)
        couplings[:, at] = row

    own.wait()
    compute(0, True)
    compute(1)
    compute(-1)
    ring_rest(3)
    compute(2)
    compute(-2)

    @pl.loop(0, 8)
    def _(dy):
        exchange_wait(1, dy)
        group = lax.rem(y + dy, 8)
        at = pl.ds(pl.multiple_of(group * 128, 128), 128)
        spread[:, at] = unpack_rows(rx1, group).T[0:NB]

    compute(3)
    compute(-3)
    ring_rest(4)
    compute(4)

    acc[NB:128] = jnp.zeros((128 - NB, J), jnp.float32)
    own_centrifugal = pick((me * NB + lax.broadcasted_iota(jnp.int32, (NB, 1), 0)) // RS)

    def pair_of(i):
        return lax.rem(y // 2 + jnp.where(i == 0, 2, jnp.where(i == 3, 0, 2 * i - 1)), 4)

    @pl.loop(0, 4)
    def _(i):
        at = pl.ds(pl.multiple_of(pair_of(i) * 256, 256), 256)
        packet = spread[:, at] + FACTOR * acc[0:NB, at]
        spread[:, at] = packet
        scaled_points[:, at] = own_centrifugal * couplings[:, at] * packet
        hel_start(lambda: hel_second(i, at))
        high, low = halves_of(packet)
        pt[0:NB, at] = high
        pt[NB : 2 * NB, at] = low

    @pl.loop(0, 8)
    def _(i):
        dy = far_first(i)
        group = lax.rem(y + dy, 8)
        pack_rows(acc[:, pl.ds(pl.multiple_of(group * 128, 128), 128)].T, tx2, group)
        exchange_start(2, group, dy)

    @pl.loop(0, 6)
    def _(i):
        at = pl.ds(pl.multiple_of(i * 256, 256), 256)
        weighted[:, at] = points_of(at, vt[:, at])

    @pl.loop(0, 4)
    def _(i):
        pair_at = pair_of(i)
        at = pl.ds(pl.multiple_of(pair_at * 256, 256), 256)
        total = back_of(weighted[...], thigh[:, at], tlow[:, at])
        hel_wait(lambda: hel_second(i, at))
        factor = own_centrifugal * couplings[:, at]
        acc[0:NB, at] = total + (factor * below_points[:, at] + above_points[:, at])
        for part in range(2):
            group = 2 * pair_at + part
            pack_rows(acc[:, pl.ds(pl.multiple_of(group * 128, 128), 128)].T, tx3, group)
            exchange_start(3, group, lax.rem(group - y + 8, 8))

    def take_back(k, out):
        @pl.loop(0, 8)
        def _(i):
            dy = far_first(i)
            exchange_wait(k, dy)
            group = lax.rem(y + dy, 8)
            for t, tile in enumerate(unpack_columns(rxs[k], group)):
                at = pl.ds(pl.multiple_of(group * 640 + 128 * t, 128), 128)
                out[:, at] = linear[:, at] + FACTOR * tile

    take_back(2, mid)
    radial_big(mid)
    local_part(mid, p1)
    take_back(3, last)

    for k in range(4):
        exchange_sent(k)
    pltpu.make_async_remote_copy(
        src_ref=tall.at[pl.ds(0, 63)], dst_ref=tall.at[pl.ds(0, 63)], send_sem=t_send, recv_sem=z_recv.at[0],
        device_id=twin, device_id_type=MESH,
    ).wait_send()


def hand_out(mid, last, mid_out, last_out):
    mid_out[...] = mid[...]
    last_out[...] = last[...]


def shards(packet_prev, packet_now, angular_table, potential, rotation, radial_weight, coupling, centrifugal):
    small_op, big_op = (jnp.asarray(a) for a in kinetic_tables())
    whole = jax.ShapeDtypeStruct((ROWS, TILES * 128), jnp.float32)
    vmem = pl.BlockSpec(memory_space=pltpu.VMEM)
    packet = (ROWS, TILES * 128)
    f32, bf16 = jnp.float32, jnp.bfloat16
    dma = pltpu.SemaphoreType.DMA
    mid, last = pl.pallas_call(
        kernel,
        out_shape=(whole, whole),
        in_specs=[vmem] * 10,
        out_specs=(vmem, vmem),
        scratch_shapes=[
            pltpu.VMEM((64, 24, J), f32),
            pltpu.VMEM((Q, J), bf16),
            pltpu.VMEM((Q, J), bf16),
            pltpu.VMEM((8, NB, 256), f32),
            pltpu.VMEM((2 * NB, J), bf16),
            pltpu.VMEM((2 * NB, Q), bf16),
            pltpu.VMEM((NB, J), f32),
            pltpu.VMEM((128, J), f32),
            *[pltpu.VMEM(packet, f32) for _ in range(5)],
            pltpu.VMEM((768, 128), f32),
            pltpu.VMEM((640, 128), f32),
            pltpu.VMEM((ROWS, 128), f32),
            pltpu.VMEM((1, J), f32),
            *[pltpu.VMEM((NB, J), f32) for _ in range(3)],
            *[pltpu.VMEM((64, 16, 128), f32) for _ in range(8)],
            dma,
            dma,
            dma((3,)),
            dma((2, 4, 4)),
            dma((8, 4)),
            dma((4,)),
            dma((4, 8)),
            dma((2,)),
            dma((2,)),
            dma((4, 2)),
            dma((4, 2)),
            pltpu.SemaphoreType.REGULAR,
            pltpu.SemaphoreType.REGULAR,
        ],
        compiler_params=pltpu.CompilerParams(collective_id=0, has_side_effects=True, vmem_limit_bytes=56 << 20),
        cost_estimate=pl.CostEstimate(flops=4 * 3 * 2 * J * Q * NB, bytes_accessed=4 << 20, transcendentals=0),
    )(
        packet_prev[0],
        packet_now[0],
        angular_table[0].T,
        potential.T,
        rotation,
        radial_weight.reshape(1, RS),
        coupling,
        centrifugal.reshape(1, RB),
        small_op,
        big_op,
    )
    mid, last = pl.pallas_call(
        hand_out, out_shape=(whole, whole), in_specs=[vmem] * 2, out_specs=(vmem, vmem)
    )(mid, last)
    return mid[None], last[None]


def solution(mesh):
    finer = Mesh(
        mesh.devices.reshape(8, 4, 2, mesh.shape["hel"]), ("grid_0", "grid_1", "grid_2", "hel")
    )
    placed = (
        P("hel", GRID, None),
        P("hel", GRID, None),
        P("hel", None, GRID),
        P(None, GRID),
        P("hel", GRID),
        P(),
        P("hel", GRID),
        P(),
    )
    return jax.shard_map(
        shards,
        mesh=finer,
        in_specs=placed,
        out_specs=(P("hel", GRID, None), P("hel", GRID, None)),
        check_vma=False,
    )
```
